32 devices in a mesh: seq: 8 (over z, x), heads: 4 (over y, core).
Axes of the slice: x: 2, y: 2, z: 4, core: 2. Of those that a mesh axis runs over, the one named last changes fastest.
Arguments:
- query_rows: bfloat16 [4096, 2048], P('seq', 'heads'), may hold values from -8 to 8
- key_rows: bfloat16 [4096, 2048], P('seq', 'heads'), may hold values from -8 to 8
- value_rows: bfloat16 [4096, 2048], P('seq', 'heads'), may hold values from -6 to 6
- doc_ids: int32 [4096], P('seq'), may hold values from 0 to 3, never falling along the last dimension, each value on 1 to 2048 neighbouring positions
- grad_out: bfloat16 [4096, 2048], P('seq', 'heads'), may hold values from -6 to 6
- out_weight: bfloat16 [2048, 2048], P('heads'), may hold values from -0.125 to 0.125
Outputs:
- grad_query: bfloat16 [4096, 2048], P('seq', 'heads')
- grad_keys: bfloat16 [4096, 2048], P('seq', 'heads')
- grad_values: bfloat16 [4096, 2048], P('seq', 'heads')
- grad_weight: float32 [2048, 2048], P('heads', 'seq')
The draws below stay inside these ranges and needn't reach their ends.
Inputs may be any that keep to these rules, and one draw needn't show every extreme that they name: `doc_ids`: Non-decreasing along the sequence; each document holds at most (2048) tokens.
All inputs are finite; a program needn't handle non-finite values.
Results may differ from the reference program's by a relative error of at most 0.02.
Values may be sent and summed in bfloat16 or wider, within the bound.
A program may use at most 256 MiB of HBM per device.

```python
import math
import jax
import jax.numpy as jnp
import numpy as np
from jax import lax

D = 2048
HEADS = 32
HD = 64
S_DEV = 512
INNER = 2048
TOKENS = 4096
N_SEQ = 8


def draw_query_rows(key, part):
    key = jax.random.fold_in(key, 3)
    result = jnp.clip(jax.random.normal(key, (TOKENS, INNER), jnp.float32), -4.0, 4.0)
    return result.astype(jnp.bfloat16)


def draw_key_rows(key, part):
    key = jax.random.fold_in(key, 5)
    result = jnp.clip(jax.random.normal(key, (TOKENS, INNER), jnp.float32), -4.0, 4.0)
    return result.astype(jnp.bfloat16)


def block_levels(stream_key, shape, shards, least, high):
    def one(axis_at, blocks):
        heights = jax.random.uniform(jax.random.fold_in(jax.random.fold_in(stream_key, 6), axis_at), (blocks,), jnp.float32, least / len(shards), high / len(shards))
        return jnp.repeat(jnp.exp(heights), shape[axis_at] // blocks).reshape((-1,) + (1,) * (len(shape) - axis_at - 1))

    level = one(*shards[0])
    for cut in shards[1:]:
        level = level * one(*cut)
    return level


def length_profile(amount, total, bound, lean):
    portions = [(1 << 20) // math.isqrt(grade ** lean) + 1 for grade in range(2, amount + 1)]
    rest, counts = total - bound - (amount - 1), [1] * (amount - 1)
    while rest > 0:
        candidates = [i for i in range(amount - 1) if counts[i] < bound]
        whole, left = sum([portions[i] for i in candidates]), rest
        for i in candidates:
            more = min(bound - counts[i], max(1, left * portions[i] // whole), rest)
            counts[i] = counts[i] + more
            rest = rest - more
    return np.array([bound] + counts)


def uneven_parts(own_key, count, total, reach, slope):
    if count == 2:
        one = jax.random.randint(own_key, (), max(1, total - reach), min(reach, total - 1) + 1)
        return jnp.stack([one, total - one])
    tallies = jnp.asarray(length_profile(count, total, reach, slope), jnp.int32)
    couples = (count - 1) // 2
    donor, receiver = tallies[1:1 + 2 * couples:2], tallies[2:2 + 2 * couples:2]
    margin = jnp.minimum(donor - 1, reach - receiver)
    passed = jax.random.randint(jax.random.fold_in(own_key, 1), (couples,), 0, 1 << 20) % (margin + 1)
    tallies = tallies.at[1:1 + 2 * couples:2].set(donor - passed).at[2:2 + 2 * couples:2].set(receiver + passed)
    return tallies[jax.random.permutation(jax.random.fold_in(own_key, 2), count)]


def normal_values(rng, extent, spread, bound, pieces=(), held_as=jnp.bfloat16):
    gain = block_levels(rng, extent, pieces, -0.22, 0.18) if pieces else 1.0
    array = jax.random.normal(rng, extent, jnp.float32) * spread * gain
    return jnp.minimum(jnp.maximum(array, -bound), bound).astype(held_as)


def setup_inputs(seed: int = 0) -> dict:
    key_of = jax.random.split(jax.random.key(seed), 7)
    query_rows = draw_query_rows(jax.random.fold_in(key_of[6], 71), 0)
    key_rows = draw_key_rows(jax.random.fold_in(key_of[6], 71), 0)
    value_rows = normal_values(key_of[2], (TOKENS, INNER), 1.0, 6.0, ((0, 8), (1, 4)))
    doc_ids = jnp.searchsorted(jnp.cumsum(uneven_parts(key_of[3], N_SEQ // 2, TOKENS, 4 * S_DEV, 0)), jnp.arange(TOKENS), side="right").astype(jnp.int32)
    grad_out = normal_values(key_of[4], (TOKENS, D), 1.0, 6.0, ((0, 8), (1, 4)))
    out_weight = normal_values(key_of[5], (INNER, D), INNER ** -0.5, 0.125, ((0, 4),))
    return {"query_rows": query_rows, "key_rows": key_rows, "value_rows": value_rows, "doc_ids": doc_ids, "grad_out": grad_out, "out_weight": out_weight}


score_scale = 0.125
very_low = -1e30


def head_slice(matrix, head_index):
    return lax.dynamic_slice_in_dim(matrix, head_index * HD, HD, 1).astype(jnp.float32)


def to_bf16(values_in):
    rounded = values_in.astype(jnp.bfloat16)
    rounded = lax.optimization_barrier(rounded)
    return rounded.astype(jnp.float32)


def reference(query_rows, key_rows, value_rows, doc_ids, grad_out, out_weight):
    positions = jnp.arange(TOKENS, dtype=jnp.int32)
    allowed = (positions[None, :] <= positions[:, None]) & (doc_ids[None, :] == doc_ids[:, None])

    def head_scores(head_index):
        queries = head_slice(query_rows, head_index)
        keyset = head_slice(key_rows, head_index)
        scores = jnp.dot(queries, keyset.T, preferred_element_type=jnp.float32) * score_scale
        return jnp.where(allowed, scores, very_low)

    def forward_head(head_index):
        scores = head_scores(head_index)
        valueset = head_slice(value_rows, head_index)
        row_max = jnp.max(scores, axis=1)
        weights = jnp.where(allowed, jnp.exp(scores - row_max[:, None]), 0.0)
        row_sum = jnp.sum(weights, axis=1)
        output = jnp.dot(to_bf16(weights), valueset, preferred_element_type=jnp.float32) / row_sum[:, None]
        return output.astype(jnp.bfloat16), row_max + jnp.log(row_sum)

    context_heads, log_totals = lax.map(forward_head, jnp.arange(HEADS, dtype=jnp.int32))
    context = jnp.transpose(context_heads, (1, 0, 2)).reshape(TOKENS, INNER)
    grad_context = jnp.dot(grad_out.astype(jnp.float32), out_weight.astype(jnp.float32).T,
                           preferred_element_type=jnp.float32).astype(jnp.bfloat16)
    grad_weight = jnp.dot(context.astype(jnp.float32).T, grad_out.astype(jnp.float32),
                          preferred_element_type=jnp.float32)

    def backward_head(inputs):
        head_index, log_total = inputs
        scores = head_scores(head_index)
        queries = head_slice(query_rows, head_index)
        keyset = head_slice(key_rows, head_index)
        valueset = head_slice(value_rows, head_index)
        grad_ctx = head_slice(grad_context, head_index)
        ctx_head = head_slice(context, head_index)
        row_delta = jnp.sum(grad_ctx * ctx_head, axis=1)
        attn_prob = jnp.where(allowed, jnp.exp(scores - log_total[:, None]), 0.0)
        grad_prob = jnp.dot(grad_ctx, valueset.T, preferred_element_type=jnp.float32)
        grad_score = to_bf16(attn_prob * (grad_prob - row_delta[:, None]))
        prob_rounded = to_bf16(attn_prob)
        query_grad = jnp.dot(grad_score, keyset, preferred_element_type=jnp.float32) * score_scale
        key_grad = jnp.dot(grad_score.T, queries, preferred_element_type=jnp.float32) * score_scale
        value_grad = jnp.dot(prob_rounded.T, grad_ctx, preferred_element_type=jnp.float32)
        return query_grad.astype(jnp.bfloat16), key_grad.astype(jnp.bfloat16), value_grad.astype(jnp.bfloat16)

    query_heads, key_heads, value_heads = lax.map(backward_head, (jnp.arange(HEADS, dtype=jnp.int32), log_totals))

    def joined(stacked):
        return jnp.transpose(stacked, (1, 0, 2)).reshape(TOKENS, INNER)

    return joined(query_heads), joined(key_heads), joined(value_heads), grad_weight
```

```python
import functools
import math

import jax
import jax.numpy as jnp
from jax import lax
from jax.experimental import pallas as pl
from jax.experimental.pallas import tpu as pltpu
from jax.sharding import PartitionSpec as P

HD = 64


score_scale = 0.125
very_low = -1e30


def shifted(value, axis, by):
    devices = lax.axis_size(axis)
    pairs = [(i, i + by) for i in range(devices) if 0 <= i + by < devices]
    return lax.ppermute(value, axis, pairs)


def per_head(matrix):
    return matrix.reshape(matrix.shape[0], matrix.shape[1] // HD, HD)


def merged(tensor):
    return jnp.transpose(tensor, (1, 0, 2)).reshape(
        tensor.shape[1], tensor.shape[0] * tensor.shape[2]
    )


def pair_scores(query_part, key_part, query_pos, key_pos, query_doc, key_doc):
    scores = (
        jnp.einsum(
            "qhd,khd->hqk",
            per_head(query_part),
            per_head(key_part),
            preferred_element_type=jnp.float32,
        )
        * score_scale
    )
    allowed = (key_pos[None, :] <= query_pos[:, None]) & (key_doc[None, :] == query_doc[:, None])
    return (scores, allowed[None])


BLOCK = 512
LOG2E = math.log2(math.e)
EXP2_SCALE = score_scale * LOG2E
MESH = pl.DeviceIdType.MESH
VMEM = pl.BlockSpec(memory_space=pltpu.VMEM)
SMEM = pl.BlockSpec(memory_space=pltpu.SMEM)
HBM = pl.BlockSpec(memory_space=pl.ANY)


def exchange_kernel(count, to_heads, with_docs, *refs):
    if with_docs:
        x_ref, doc_ref, o_ref, all_doc_ref, send, recv, local, dsend, drecv = refs
    else:
        x_ref, o_ref, send, recv, local = refs
    me = lax.axis_index("seq")
    barrier = pltpu.get_barrier_semaphore()
    for step in range(1, count):
        pl.semaphore_signal(
            barrier, inc=1, device_id={"seq": lax.rem(me + step, count)}, device_id_type=MESH
        )
    pl.semaphore_wait(barrier, count - 1)
    cols = x_ref.shape[2] if to_heads else x_ref.shape[2] // count

    def source(owner):
        if to_heads:
            return x_ref.at[:, pl.ds(pl.multiple_of(owner * HD, HD), HD), :]
        return x_ref.at[:, :, pl.ds(pl.multiple_of(owner * cols, cols), cols)]

    def target():
        if to_heads:
            return o_ref.at[:, :, pl.ds(pl.multiple_of(me * cols, cols), cols)]
        return o_ref.at[:, pl.ds(pl.multiple_of(me * HD, HD), HD), :]

    own = pltpu.make_async_copy(source(me), target(), local.at[0])
    own.start()
    copies = []
    if with_docs:
        own_doc = pltpu.make_async_copy(doc_ref, all_doc_ref.at[me], local.at[1])
        own_doc.start()
        for step in range(1, count):
            peer = lax.rem(me + step, count)
            copies.append(
                pltpu.make_async_remote_copy(
                    src_ref=doc_ref,
                    dst_ref=all_doc_ref.at[me],
                    send_sem=dsend.at[step],
                    recv_sem=drecv.at[step],
                    device_id={"seq": peer},
                    device_id_type=MESH,
                )
            )
    for step in range(1, count):
        peer = lax.rem(me + step, count)
        copies.append(
            pltpu.make_async_remote_copy(
                src_ref=source(peer),
                dst_ref=target(),
                send_sem=send.at[step],
                recv_sem=recv.at[step],
                device_id={"seq": peer},
                device_id_type=MESH,
            )
        )
    for copy in copies:
        copy.start()
    own.wait()
    if with_docs:
        own_doc.wait()
    for copy in copies:
        copy.wait()


def exchange(x, count, to_heads, collective_id, docs=None):
    kinds, rows, cols = x.shape
    shape = (kinds, rows // count, cols * count) if to_heads else (kinds, rows * count, cols // count)
    out_shape = [jax.ShapeDtypeStruct(shape, x.dtype)]
    operands = [x]
    sems = [pltpu.SemaphoreType.DMA((count,))] * 2 + [pltpu.SemaphoreType.DMA((2,))]
    if docs is not None:
        docs = docs.reshape(-1, 128)
        out_shape.append(jax.ShapeDtypeStruct((count,) + docs.shape, docs.dtype))
        operands.append(docs)
        sems += [pltpu.SemaphoreType.DMA((count,))] * 2
    outs = pl.pallas_call(
        functools.partial(exchange_kernel, count, to_heads, docs is not None),
        out_shape=out_shape,
        in_specs=[HBM] * len(operands),
        out_specs=[HBM] * len(out_shape),
        scratch_shapes=sems,
        compiler_params=pltpu.CompilerParams(collective_id=collective_id, has_side_effects=True),
        cost_estimate=pl.CostEstimate(
            flops=0, bytes_accessed=100 * x.size * x.dtype.itemsize, transcendentals=0
        ),
    )(*operands)
    return outs


def block_at(index):
    return pl.ds(pl.multiple_of(index * BLOCK, BLOCK), BLOCK)


def rows_of(cols_ref, slot, rows_ref, blocks):
    def step(b, _):
        at = block_at(b)
        rows_ref[at, :] = cols_ref[slot, :, at].T
        return 0

    lax.fori_loop(0, blocks, step, 0)


def scaled_scores(key_rows, query_cols, first_key, first_query, start, masked):
    scores = jnp.dot(key_rows, query_cols, preferred_element_type=jnp.float32) * EXP2_SCALE
    if masked:
        key_pos = first_key + lax.broadcasted_iota(jnp.int32, scores.shape, 0)
        query_pos = first_query + lax.broadcasted_iota(jnp.int32, (1, scores.shape[1]), 1)
        allowed = (key_pos <= query_pos) & (key_pos >= start)
        scores = jnp.where(allowed, scores, very_low)
    return scores


def forward_kernel(low_ref, full_ref, start_ref, qkv_ref, ctx_ref, total_ref, key_rows):
    blocks = qkv_ref.shape[2] // BLOCK
    rows_of(qkv_ref, 1, key_rows, blocks)

    def query_block(j, _):
        cols = block_at(j)
        query_cols = qkv_ref[0, :, cols]
        start = start_ref[:, cols]

        def term(i, masked):
            keys = block_at(i)
            return scaled_scores(
                key_rows[keys, :], query_cols, i * BLOCK, j * BLOCK, start, masked
            ), qkv_ref[2, :, keys]

        scores, values = term(j, True)
        run_max = jnp.max(scores, axis=0, keepdims=True)
        prob = jnp.exp2(scores - run_max)
        run_sum = jnp.sum(prob, axis=0, keepdims=True)
        acc = jnp.dot(values, prob.astype(jnp.bfloat16), preferred_element_type=jnp.float32)

        def step(masked, i, state):
            run_max, run_sum, acc = state
            scores, values = term(i, masked)
            new_max = jnp.maximum(run_max, jnp.max(scores, axis=0, keepdims=True))
            factor = jnp.exp2(run_max - new_max)
            prob = jnp.exp2(scores - new_max)
            run_sum = run_sum * factor + jnp.sum(prob, axis=0, keepdims=True)
            acc = acc * factor + jnp.dot(
                values, prob.astype(jnp.bfloat16), preferred_element_type=jnp.float32
            )
            return new_max, run_sum, acc

        low, full = low_ref[j], full_ref[j]
        state = (run_max, run_sum, acc)
        state = lax.fori_loop(low, full, functools.partial(step, True), state)
        state = lax.fori_loop(full, j, functools.partial(step, False), state)
        run_max, run_sum, acc = state
        ctx_ref[0, :, cols] = (acc / run_sum).astype(jnp.bfloat16)
        total_ref[:, cols] = run_max + jnp.log(run_sum) * LOG2E
        return 0

    lax.fori_loop(0, blocks, query_block, 0)


def nt_dot(a, b):
    return lax.dot_general(a, b, (((1,), (1,)), ((), ())), preferred_element_type=jnp.float32)


def backward_kernel(
    low_ref, full_ref, start_ref, qkv_ref, ctx_ref, dctx_ref, total_ref, out_ref,
    key_rows, value_rows, key_acc, value_acc,
):
    blocks = qkv_ref.shape[2] // BLOCK
    rows_of(qkv_ref, 1, key_rows, blocks)
    rows_of(qkv_ref, 2, value_rows, blocks)

    def query_block(j, _):
        cols = block_at(j)
        query_cols = qkv_ref[0, :, cols]
        grad_cols = dctx_ref[0, :, cols]
        start = start_ref[:, cols]
        total = total_ref[:, cols]
        delta = jnp.sum(
            grad_cols.astype(jnp.float32) * ctx_ref[0, :, cols].astype(jnp.float32),
            axis=0,
            keepdims=True,
        )

        def term(i, masked):
            keys = block_at(i)
            scores = scaled_scores(
                key_rows[keys, :], query_cols, i * BLOCK, j * BLOCK, start, masked
            )
            prob = jnp.exp2(scores - total)
            grad_prob = jnp.dot(
                value_rows[keys, :], grad_cols, preferred_element_type=jnp.float32
            )
            grad_score = (prob * (grad_prob - delta)).astype(jnp.bfloat16)
            value_term = nt_dot(grad_cols, prob.astype(jnp.bfloat16))
            key_term = nt_dot(query_cols, grad_score)
            query_term = jnp.dot(
                qkv_ref[1, :, keys], grad_score, preferred_element_type=jnp.float32
            )
            return keys, key_term, value_term, query_term

        keys, key_term, value_term, query_acc = term(j, True)
        key_acc[:, keys] = key_term
        value_acc[:, keys] = value_term

        def step(masked, i, query_acc):
            keys, key_term, value_term, query_term = term(i, masked)
            key_acc[:, keys] += key_term
            value_acc[:, keys] += value_term
            return query_acc + query_term

        low, full = low_ref[j], full_ref[j]
        query_acc = lax.fori_loop(low, full, functools.partial(step, True), query_acc)
        query_acc = lax.fori_loop(full, j, functools.partial(step, False), query_acc)
        out_ref[0, :, cols] = (query_acc * score_scale).astype(jnp.bfloat16)
        return 0

    lax.fori_loop(0, blocks, query_block, 0)

    def finish(b, _):
        at = block_at(b)
        out_ref[1, :, at] = (key_acc[:, at] * score_scale).astype(jnp.bfloat16)
        out_ref[2, :, at] = value_acc[:, at].astype(jnp.bfloat16)
        return 0

    lax.fori_loop(0, blocks, finish, 0)


def attention_forward(low, full, start, qkv):
    tokens = qkv.shape[2]
    return pl.pallas_call(
        forward_kernel,
        out_shape=[
            jax.ShapeDtypeStruct((1, HD, tokens), jnp.bfloat16),
            jax.ShapeDtypeStruct((1, tokens), jnp.float32),
        ],
        in_specs=[SMEM, SMEM, VMEM, VMEM],
        out_specs=[VMEM, VMEM],
        scratch_shapes=[pltpu.VMEM((tokens, HD), jnp.bfloat16)],
        compiler_params=pltpu.CompilerParams(vmem_limit_bytes=40 << 20),
        cost_estimate=pl.CostEstimate(
            flops=tokens * tokens * HD * 2, bytes_accessed=3 * qkv.size, transcendentals=0
        ),
    )(low, full, start, qkv)


def attention_backward(low, full, start, qkv, ctx, dctx, total):
    tokens = qkv.shape[2]
    return pl.pallas_call(
        backward_kernel,
        out_shape=jax.ShapeDtypeStruct((3, HD, tokens), jnp.bfloat16),
        in_specs=[SMEM, SMEM, VMEM, VMEM, VMEM, VMEM, VMEM],
        out_specs=VMEM,
        scratch_shapes=[pltpu.VMEM((tokens, HD), jnp.bfloat16)] * 2
        + [pltpu.VMEM((HD, tokens), jnp.float32)] * 2,
        compiler_params=pltpu.CompilerParams(vmem_limit_bytes=40 << 20),
        cost_estimate=pl.CostEstimate(
            flops=tokens * tokens * HD * 5, bytes_accessed=6 * qkv.size, transcendentals=0
        ),
    )(low, full, start, qkv, ctx, dctx, total)


def doc_ranges(docs):
    tokens = docs.shape[0]
    ids = jnp.arange(8, dtype=jnp.int32)
    begins = jnp.sum((docs[None, :] < ids[:, None]).astype(jnp.int32), axis=1)
    start = jnp.sum(jnp.where(docs[None, :] == ids[:, None], begins[:, None], 0), axis=0)
    blocks = tokens // BLOCK
    grouped = start.reshape(blocks, BLOCK)
    low = grouped[:, 0] // BLOCK
    full = (grouped[:, BLOCK - 1] + BLOCK - 1) // BLOCK
    full = jnp.minimum(full, jnp.arange(blocks, dtype=jnp.int32))
    return low, full, start[None]


def head_shards(query_rows, key_rows, value_rows, doc_ids, grad_out, out_weight):
    count = lax.axis_size("seq")
    full_grad = lax.all_gather(grad_out, "heads", axis=1, tiled=True)
    stacked = jnp.stack([query_rows.T, key_rows.T, value_rows.T])
    qkv, docs = exchange(stacked, count, True, 0, doc_ids)
    low, full, start = doc_ranges(docs.reshape(-1))
    grad_context = nt_dot(out_weight, full_grad).astype(jnp.bfloat16)
    (dctx,) = exchange(grad_context[None], count, True, 1)
    ctx, total = attention_forward(low, full, start, qkv)
    (context,) = exchange(ctx, count, False, 2)
    weight_term = jnp.dot(context[0], full_grad, preferred_element_type=jnp.float32)
    grad_weight = lax.psum_scatter(
        weight_term.astype(jnp.bfloat16), "seq", scatter_dimension=1, tiled=True
    ).astype(jnp.float32)
    grads = attention_backward(low, full, start, qkv, ctx, dctx, total)
    (back,) = exchange(grads, count, False, 3)
    return (back[0].T, back[1].T, back[2].T, grad_weight)


def ring_shards(query_rows, key_rows, value_rows, doc_ids, grad_out, out_weight):
    shard_rows = query_rows.shape[0]
    inner_cols = query_rows.shape[1]
    head_count = inner_cols // HD
    seq_count = lax.axis_size("seq")
    total_rows = shard_rows * seq_count
    first_row = lax.axis_index("seq") * shard_rows
    query_pos = first_row + jnp.arange(shard_rows, dtype=jnp.int32)
    all_docs = lax.all_gather(doc_ids, "seq", axis=0, tiled=True)

    def key_info(offset, length):
        key_pos = offset + jnp.arange(length, dtype=jnp.int32)
        inside = (key_pos >= 0) & (key_pos < total_rows)
        key_doc = lax.dynamic_slice_in_dim(all_docs, offset, length, 0)
        key_doc = jnp.where(inside, key_doc, -1)
        return (key_pos, key_doc)

    init_fwd = (
        jnp.full((head_count, shard_rows), very_low, jnp.float32),
        jnp.zeros((head_count, shard_rows), jnp.float32),
        jnp.zeros((head_count, shard_rows, HD), jnp.float32),
    )
    reach = min(4, seq_count - 1)
    near_keys = []
    near_keys.append((0, key_rows, value_rows))
    for distance in range(1, reach + 1):
        key_in, value_in = shifted((key_rows, value_rows), "seq", distance)
        near_keys.append((distance, key_in, value_in))
    running = init_fwd
    for distance, key_part, value_part in near_keys:
        forward_key_pos, forward_key_doc = key_info(
            first_row - distance * shard_rows, key_part.shape[0]
        )
        forward_run_max, forward_run_sum, forward_run_acc = running
        forward_scores, forward_allowed = pair_scores(
            query_rows, key_part, query_pos, forward_key_pos, doc_ids, forward_key_doc
        )
        forward_scores = jnp.where(forward_allowed, forward_scores, very_low)
        new_max = jnp.maximum(forward_run_max, jnp.max(forward_scores, axis=2))
        forward_attn_prob = jnp.where(
            forward_allowed, jnp.exp(forward_scores - new_max[:, :, None]), 0.0
        )
        factor = jnp.exp(forward_run_max - new_max)
        forward_run_sum = forward_run_sum * factor + jnp.sum(forward_attn_prob, axis=2)
        forward_run_acc = forward_run_acc * factor[:, :, None] + jnp.einsum(
            "hqk,khd->hqd",
            forward_attn_prob.astype(jnp.bfloat16),
            per_head(value_part),
            preferred_element_type=jnp.float32,
        )
        running = (new_max, forward_run_sum, forward_run_acc)
    run_max, run_sum, run_acc = running
    context = merged(run_acc / run_sum[:, :, None]).astype(jnp.bfloat16)
    log_total = run_max + jnp.log(run_sum)
    full_grad = lax.all_gather(grad_out, "heads", axis=1, tiled=True)
    grad_context = lax.dot_general(
        full_grad, out_weight, (((1,), (1,)), ((), ())), preferred_element_type=jnp.float32
    ).astype(jnp.bfloat16)
    weight_term = lax.dot_general(
        context, full_grad, (((0,), (0,)), ((), ())), preferred_element_type=jnp.float32
    )
    grad_weight = lax.psum_scatter(
        weight_term.astype(jnp.bfloat16), "seq", scatter_dimension=1, tiled=True
    ).astype(jnp.float32)
    row_delta = jnp.transpose(
        jnp.sum(
            per_head(grad_context).astype(jnp.float32) * per_head(context).astype(jnp.float32),
            axis=2,
        )
    )

    def owner_core(totals, query_part, grad_part, part_total, part_delta, offset):
        piece_rows = query_part.shape[0]
        piece_pos, piece_doc = key_info(offset, piece_rows)
        key_grad, value_grad = totals
        scores, allowed = pair_scores(
            query_part, key_rows, piece_pos, query_pos, piece_doc, doc_ids
        )
        attn_prob = jnp.where(allowed, jnp.exp(scores - part_total[:, :, None]), 0.0)
        grad_prob = jnp.einsum(
            "qhd,khd->hqk",
            per_head(grad_part),
            per_head(value_rows),
            preferred_element_type=jnp.float32,
        )
        grad_score = attn_prob * (grad_prob - part_delta[:, :, None])
        key_grad = key_grad + jnp.einsum(
            "hqk,qhd->hkd",
            grad_score.astype(jnp.bfloat16),
            per_head(query_part),
            preferred_element_type=jnp.float32,
        )
        value_grad = value_grad + jnp.einsum(
            "hqk,qhd->hkd",
            attn_prob.astype(jnp.bfloat16),
            per_head(grad_part),
            preferred_element_type=jnp.float32,
        )
        return (key_grad, value_grad)

    init_grad = jnp.zeros((head_count, shard_rows, HD), jnp.float32)
    query_acc = init_grad
    for distance, key_part, value_part in near_keys:
        query_key_pos, query_key_doc = key_info(
            first_row - distance * shard_rows, key_part.shape[0]
        )
        query_scores, query_allowed = pair_scores(
            query_rows, key_part, query_pos, query_key_pos, doc_ids, query_key_doc
        )
        query_attn_prob = jnp.where(
            query_allowed, jnp.exp(query_scores - log_total[:, :, None]), 0.0
        )
        query_grad_prob = jnp.einsum(
            "qhd,khd->hqk",
            per_head(grad_context),
            per_head(value_part),
            preferred_element_type=jnp.float32,
        )
        query_grad_score = query_attn_prob * (query_grad_prob - row_delta[:, :, None])
        query_acc = query_acc + jnp.einsum(
            "hqk,khd->hqd",
            query_grad_score.astype(jnp.bfloat16),
            per_head(key_part),
            preferred_element_type=jnp.float32,
        )
    owner_totals = owner_core(
        (init_grad, init_grad), query_rows, grad_context, log_total, row_delta, first_row
    )
    for distance in range(1, reach + 1):
        query_in, grad_in = shifted((query_rows, grad_context), "seq", -distance)
        total_in, delta_in = shifted((log_total, row_delta), "seq", -distance)
        owner_totals = owner_core(
            owner_totals, query_in, grad_in, total_in, delta_in, first_row + distance * shard_rows
        )
    key_acc, value_acc = owner_totals
    grad_keys = (merged(key_acc) * score_scale).astype(jnp.bfloat16)
    grad_values = merged(value_acc).astype(jnp.bfloat16)
    grad_query = (merged(query_acc) * score_scale).astype(jnp.bfloat16)
    return (grad_query, grad_keys, grad_values, grad_weight)


def solution(mesh):
    def shards(query_rows, *others):
        heads_here = query_rows.shape[1] // HD
        if heads_here == mesh.shape["seq"] and query_rows.shape[0] % 512 == 0:
            return head_shards(query_rows, *others)
        return ring_shards(query_rows, *others)

    return jax.shard_map(
        shards,
        mesh=mesh,
        in_specs=(
            P("seq", "heads"),
            P("seq", "heads"),
            P("seq", "heads"),
            P("seq"),
            P("seq", "heads"),
            P("heads", None),
        ),
        out_specs=(P("seq", "heads"), P("seq", "heads"), P("seq", "heads"), P("heads", "seq")),
        check_vma=False,
    )
```

```python
import functools
import math

import jax
import jax.numpy as jnp
from jax import lax
from jax.experimental import pallas as pl
from jax.experimental.pallas import tpu as pltpu
from jax.sharding import PartitionSpec as P

HD = 64


score_scale = 0.125
very_low = -1e30


def shifted(value, axis, by):
    devices = lax.axis_size(axis)
    pairs = [(i, i + by) for i in range(devices) if 0 <= i + by < devices]
    return lax.ppermute(value, axis, pairs)


def per_head(matrix):
    return matrix.reshape(matrix.shape[0], matrix.shape[1] // HD, HD)


def merged(tensor):
    return jnp.transpose(tensor, (1, 0, 2)).reshape(
        tensor.shape[1], tensor.shape[0] * tensor.shape[2]
    )


def pair_scores(query_part, key_part, query_pos, key_pos, query_doc, key_doc):
    scores = (
        jnp.einsum(
            "qhd,khd->hqk",
            per_head(query_part),
            per_head(key_part),
            preferred_element_type=jnp.float32,
        )
        * score_scale
    )
    allowed = (key_pos[None, :] <= query_pos[:, None]) & (key_doc[None, :] == query_doc[:, None])
    return (scores, allowed[None])


BLOCK = 512
LOG2E = math.log2(math.e)
EXP2_SCALE = score_scale * LOG2E
MESH = pl.DeviceIdType.MESH
VMEM = pl.BlockSpec(memory_space=pltpu.VMEM)
SMEM = pl.BlockSpec(memory_space=pltpu.SMEM)
HBM = pl.BlockSpec(memory_space=pl.ANY)


def mod(a, b):
    return lax.rem(a, jnp.int32(b))


def div(a, b):
    return lax.div(a, jnp.int32(b))


def greet(count, heads):
    me = lax.axis_index("seq")
    mine = lax.axis_index("heads")
    barrier = pltpu.get_barrier_semaphore()
    for step in range(1, count):
        pl.semaphore_signal(
            barrier, inc=1, device_id={"seq": mod(me + step, count)}, device_id_type=MESH
        )
    for step in range(1, heads):
        pl.semaphore_signal(
            barrier, inc=1, device_id={"heads": mod(mine + step, heads)}, device_id_type=MESH
        )
    pl.semaphore_wait(barrier, count - 1 + heads - 1)


def remote(src, dst, send, recv, slot, axis, peer):
    return pltpu.make_async_remote_copy(
        src_ref=src,
        dst_ref=dst,
        send_sem=send.at[slot],
        recv_sem=recv.at[slot],
        device_id={axis: peer},
        device_id_type=MESH,
    )


def head_rows(owner):
    return pl.ds(pl.multiple_of(owner * HD, HD), HD)


def token_cols(owner, cols):
    return pl.ds(pl.multiple_of(owner * cols, cols), cols)


def gather_kernel(
    count, heads, x_ref, doc_ref, grad_ref, weight_ref,
    qkv_ref, all_doc_ref, dctx_ref, full_ref,
    grads, dctx, xsend, xrecv, dsend, drecv, gsend, grecv, csend, crecv, local,
):
    me = lax.axis_index("seq")
    mine = lax.axis_index("heads")
    cols = x_ref.shape[2]
    width = grad_ref.shape[1]
    greet(count, heads)
    here = token_cols(me, cols)
    own = [
        pltpu.make_async_copy(grad_ref, grads.at[mine], local.at[0]),
        pltpu.make_async_copy(doc_ref, all_doc_ref.at[me], local.at[1]),
        pltpu.make_async_copy(x_ref.at[:, head_rows(me), :], qkv_ref.at[:, :, here], local.at[2]),
    ]
    for copy in own:
        copy.start()
    wide = [
        remote(grad_ref, grads.at[mine], gsend, grecv, step, "heads", mod(mine + step, heads))
        for step in range(1, heads)
    ]
    peers = [mod(me + step, count) for step in range(1, count)]
    rest = [
        remote(doc_ref, all_doc_ref.at[me], dsend, drecv, step, "seq", peer)
        for step, peer in enumerate(peers)
    ] + [
        remote(
            x_ref.at[:, head_rows(peer), :], qkv_ref.at[:, :, here], xsend, xrecv, step, "seq", peer
        )
        for step, peer in enumerate(peers)
    ]
    for copy in wide + rest:
        copy.start()
    own[0].wait()
    for copy in wide:
        copy.wait()
    keep = pltpu.make_async_copy(grads, full_ref, local.at[0])
    keep.start()
    total = None
    for part in range(heads):
        term = nt_dot(weight_ref[:, part * width : (part + 1) * width], grads[part])
        total = term if total is None else total + term
    dctx[...] = total.astype(jnp.bfloat16)
    last = [
        remote(dctx.at[head_rows(peer), :], dctx_ref.at[0, :, here], csend, crecv, step, "seq", peer)
        for step, peer in enumerate(peers)
    ]
    for copy in last:
        copy.start()
    own_dctx = pltpu.make_async_copy(dctx.at[head_rows(me), :], dctx_ref.at[0, :, here], local.at[3])
    own_dctx.start()
    for copy in own[1:] + rest + last:
        copy.wait()
    own_dctx.wait()
    keep.wait()


def gather(x, docs, grad_out, weight, count, heads):
    kinds, rows, cols = x.shape
    docs = docs.reshape(-1, 128)
    dma = pltpu.SemaphoreType.DMA
    return pl.pallas_call(
        functools.partial(gather_kernel, count, heads),
        out_shape=[
            jax.ShapeDtypeStruct((kinds, rows // count, cols * count), x.dtype),
            jax.ShapeDtypeStruct((count,) + docs.shape, docs.dtype),
            jax.ShapeDtypeStruct((1, rows // count, cols * count), x.dtype),
            jax.ShapeDtypeStruct((heads,) + grad_out.shape, grad_out.dtype),
        ],
        in_specs=[HBM, HBM, HBM, VMEM],
        out_specs=[HBM] * 4,
        scratch_shapes=[
            pltpu.VMEM((heads,) + grad_out.shape, grad_out.dtype),
            pltpu.VMEM((rows, cols), x.dtype),
        ]
        + [dma((count,))] * 4
        + [dma((heads,))] * 2
        + [dma((count,))] * 2
        + [dma((4,))],
        compiler_params=pltpu.CompilerParams(
            collective_id=0, has_side_effects=True, vmem_limit_bytes=40 << 20
        ),
    )(x, docs, grad_out, weight)


def return_kernel(
    count, x_ref, full_ref, back_ref, out_ref,
    ctx, own_sum, xout, xin, pout, pin, cout, cin,
    ksend, krecv, gsend, grecv, xsend, xrecv, psend, precv, csend, crecv, local,
):
    me = lax.axis_index("seq")
    z, x = div(me, 2), mod(me, 2)
    depth = count // 2
    cols = x_ref.shape[2] // count
    half = own_sum.shape[2]
    greet(count, 1)
    here = head_rows(me)
    own_ctx = pltpu.make_async_copy(
        x_ref.at[3, :, token_cols(me, cols)], ctx.at[here, :], local.at[0]
    )
    own_back = pltpu.make_async_copy(
        x_ref.at[0:3, :, token_cols(me, cols)], back_ref.at[:, here, :], local.at[1]
    )
    peers = [mod(me + step, count) for step in range(1, count)]
    first = [
        remote(x_ref.at[3, :, token_cols(peer, cols)], ctx.at[here, :], ksend, krecv, step, "seq", peer)
        for step, peer in enumerate(peers)
    ]
    grads = [
        remote(
            x_ref.at[0:3, :, token_cols(peer, cols)], back_ref.at[:, here, :],
            gsend, grecv, step, "seq", peer,
        )
        for step, peer in enumerate(peers)
    ]
    own_ctx.start()
    for copy in first + grads:
        copy.start()
    own_back.start()
    own_ctx.wait()
    for copy in first:
        copy.wait()

    def product(part, side):
        at = pl.ds(pl.multiple_of(side * half, half), half)
        return jnp.dot(ctx[...], full_ref[part, :, at], preferred_element_type=jnp.float32)

    across = []
    for part in range(depth):
        xout[part] = product(part, 1 - x).astype(jnp.bfloat16)
        copy = remote(
            xout.at[part], xin.at[part], xsend, xrecv, part, "seq", z * 2 + 1 - x
        )
        copy.start()
        across.append(copy)
    for part in range(depth):
        own_sum[part] = product(part, x)
    for part in range(depth):
        across[part].wait()
        own_sum[part] += xin[part].astype(jnp.float32)
    pair = z + 1 - 2 * mod(z, 2)
    far = mod(z + 2, 4)
    pair_far = mod(pair + 2, 4)
    near = []
    for slot, block in enumerate((pair_far, pair)):
        pout[slot] = own_sum[block].astype(jnp.bfloat16)
        copy = remote(pout.at[slot], pin.at[slot], psend, precv, slot, "seq", pair * 2 + x)
        copy.start()
        near.append(copy)
    near[0].wait()
    cout[...] = (own_sum[far] + pin[0].astype(jnp.float32)).astype(jnp.bfloat16)
    cross = remote(cout, cin, csend, crecv, 0, "seq", far * 2 + x)
    cross.start()
    near[1].wait()
    cross.wait()
    out_ref[...] = own_sum[z] + pin[1].astype(jnp.float32) + cin[...].astype(jnp.float32)
    own_back.wait()
    for copy in grads:
        copy.wait()


def give_back(x, full, count):
    kinds, rows, tokens = x.shape
    inner, cols = rows * count, tokens // count
    depth = count // 2
    half = full.shape[2] // 2
    dma = pltpu.SemaphoreType.DMA
    bf16 = jnp.bfloat16
    block = (inner, half)
    return pl.pallas_call(
        functools.partial(return_kernel, count),
        out_shape=[
            jax.ShapeDtypeStruct((kinds - 1, inner, cols), x.dtype),
            jax.ShapeDtypeStruct(block, jnp.float32),
        ],
        in_specs=[HBM, VMEM],
        out_specs=[HBM, VMEM],
        scratch_shapes=[
            pltpu.VMEM((inner, cols), bf16),
            pltpu.VMEM((depth,) + block, jnp.float32),
            pltpu.VMEM((depth,) + block, bf16),
            pltpu.VMEM((depth,) + block, bf16),
            pltpu.VMEM((2,) + block, bf16),
            pltpu.VMEM((2,) + block, bf16),
            pltpu.VMEM(block, bf16),
            pltpu.VMEM(block, bf16),
        ]
        + [dma((count,))] * 4
        + [dma((depth,))] * 2
        + [dma((2,))] * 2
        + [dma((1,))] * 2
        + [dma((2,))],
        compiler_params=pltpu.CompilerParams(
            collective_id=1, has_side_effects=True, vmem_limit_bytes=40 << 20
        ),
    )(x, full)


def nt_dot(a, b):
    return lax.dot_general(a, b, (((1,), (1,)), ((), ())), preferred_element_type=jnp.float32)


def block_at(index):
    return pl.ds(pl.multiple_of(index * BLOCK, BLOCK), BLOCK)


def rows_of(cols_ref, slot, rows_ref, blocks):
    def step(b, _):
        at = block_at(b)
        rows_ref[at, :] = cols_ref[slot, :, at].T
        return 0

    lax.fori_loop(0, blocks, step, 0)


def scaled_scores(key_rows, query_cols, first_key, first_query, start, masked):
    scores = jnp.dot(key_rows, query_cols, preferred_element_type=jnp.float32) * EXP2_SCALE
    if masked:
        key_pos = first_key + lax.broadcasted_iota(jnp.int32, scores.shape, 0)
        query_pos = first_query + lax.broadcasted_iota(jnp.int32, (1, scores.shape[1]), 1)
        allowed = (key_pos <= query_pos) & (key_pos >= start)
        scores = jnp.where(allowed, scores, very_low)
    return scores


def attention_kernel(
    low_ref, full_ref, start_ref, qkv_ref, dctx_ref, out_ref,
    key_rows, value_rows, key_acc, value_acc,
):
    blocks = qkv_ref.shape[2] // BLOCK
    rows_of(qkv_ref, 1, key_rows, blocks)
    rows_of(qkv_ref, 2, value_rows, blocks)

    def query_block(j, _):
        cols = block_at(j)
        query_cols = qkv_ref[0, :, cols]
        start = start_ref[:, cols]
        low, full = low_ref[j], full_ref[j]

        def scores_of(i, masked):
            return scaled_scores(
                key_rows[block_at(i), :], query_cols, i * BLOCK, j * BLOCK, start, masked
            )

        scores = scores_of(j, True)
        run_max = jnp.max(scores, axis=0, keepdims=True)
        prob = jnp.exp2(scores - run_max)
        run_sum = jnp.sum(prob, axis=0, keepdims=True)
        acc = jnp.dot(
            qkv_ref[2, :, cols], prob.astype(jnp.bfloat16), preferred_element_type=jnp.float32
        )

        def forward(masked, i, state):
            run_max, run_sum, acc = state
            scores = scores_of(i, masked)
            new_max = jnp.maximum(run_max, jnp.max(scores, axis=0, keepdims=True))
            factor = jnp.exp2(run_max - new_max)
            prob = jnp.exp2(scores - new_max)
            run_sum = run_sum * factor + jnp.sum(prob, axis=0, keepdims=True)
            acc = acc * factor + jnp.dot(
                qkv_ref[2, :, block_at(i)],
                prob.astype(jnp.bfloat16),
                preferred_element_type=jnp.float32,
            )
            return new_max, run_sum, acc

        state = (run_max, run_sum, acc)
        state = lax.fori_loop(low, full, functools.partial(forward, True), state)
        state = lax.fori_loop(full, j, functools.partial(forward, False), state)
        run_max, run_sum, acc = state
        context = (acc / run_sum).astype(jnp.bfloat16)
        out_ref[3, :, cols] = context
        total = run_max + jnp.log(run_sum) * LOG2E
        grad_cols = dctx_ref[0, :, cols]
        delta = jnp.sum(
            grad_cols.astype(jnp.float32) * context.astype(jnp.float32), axis=0, keepdims=True
        )

        def backward(i, masked):
            keys = block_at(i)
            prob = jnp.exp2(scores_of(i, masked) - total)
            grad_prob = jnp.dot(
                value_rows[keys, :], grad_cols, preferred_element_type=jnp.float32
            )
            grad_score = (prob * (grad_prob - delta)).astype(jnp.bfloat16)
            value_term = nt_dot(grad_cols, prob.astype(jnp.bfloat16))
            key_term = nt_dot(query_cols, grad_score)
            query_term = jnp.dot(
                qkv_ref[1, :, keys], grad_score, preferred_element_type=jnp.float32
            )
            return keys, key_term, value_term, query_term

        keys, key_term, value_term, query_acc = backward(j, True)
        key_acc[:, keys] = key_term
        value_acc[:, keys] = value_term

        def step(masked, i, query_acc):
            keys, key_term, value_term, query_term = backward(i, masked)
            key_acc[:, keys] += key_term
            value_acc[:, keys] += value_term
            return query_acc + query_term

        query_acc = lax.fori_loop(low, full, functools.partial(step, True), query_acc)
        query_acc = lax.fori_loop(full, j, functools.partial(step, False), query_acc)
        out_ref[0, :, cols] = (query_acc * score_scale).astype(jnp.bfloat16)
        return 0

    lax.fori_loop(0, blocks, query_block, 0)

    def finish(b, _):
        at = block_at(b)
        out_ref[1, :, at] = (key_acc[:, at] * score_scale).astype(jnp.bfloat16)
        out_ref[2, :, at] = value_acc[:, at].astype(jnp.bfloat16)
        return 0

    lax.fori_loop(0, blocks, finish, 0)


def attention(low, full, start, qkv, dctx):
    tokens = qkv.shape[2]
    return pl.pallas_call(
        attention_kernel,
        out_shape=jax.ShapeDtypeStruct((4, HD, tokens), jnp.bfloat16),
        in_specs=[SMEM, SMEM, VMEM, VMEM, VMEM],
        out_specs=VMEM,
        scratch_shapes=[pltpu.VMEM((tokens, HD), jnp.bfloat16)] * 2
        + [pltpu.VMEM((HD, tokens), jnp.float32)] * 2,
        compiler_params=pltpu.CompilerParams(vmem_limit_bytes=40 << 20),
    )(low, full, start, qkv, dctx)


def doc_ranges(docs):
    tokens = docs.shape[0]
    ids = jnp.arange(8, dtype=jnp.int32)
    begins = jnp.sum((docs[None, :] < ids[:, None]).astype(jnp.int32), axis=1)
    start = jnp.sum(jnp.where(docs[None, :] == ids[:, None], begins[:, None], 0), axis=0)
    blocks = tokens // BLOCK
    grouped = start.reshape(blocks, BLOCK)
    low = grouped[:, 0] // BLOCK
    full = (grouped[:, BLOCK - 1] + BLOCK - 1) // BLOCK
    full = jnp.minimum(full, jnp.arange(blocks, dtype=jnp.int32))
    return low, full, start[None]


def head_shards(query_rows, key_rows, value_rows, doc_ids, grad_out, out_weight):
    count = lax.axis_size("seq")
    stacked = jnp.stack([query_rows.T, key_rows.T, value_rows.T])
    qkv, docs, dctx, full_grad = gather(
        stacked, doc_ids, grad_out, out_weight, count, lax.axis_size("heads")
    )
    low, full, start = doc_ranges(docs.reshape(-1))
    results = attention(low, full, start, qkv, dctx)
    back, grad_weight = give_back(results, full_grad, count)
    return (back[0].T, back[1].T, back[2].T, grad_weight)


def ring_shards(query_rows, key_rows, value_rows, doc_ids, grad_out, out_weight):
    shard_rows = query_rows.shape[0]
    inner_cols = query_rows.shape[1]
    head_count = inner_cols // HD
    seq_count = lax.axis_size("seq")
    total_rows = shard_rows * seq_count
    first_row = lax.axis_index("seq") * shard_rows
    query_pos = first_row + jnp.arange(shard_rows, dtype=jnp.int32)
    all_docs = lax.all_gather(doc_ids, "seq", axis=0, tiled=True)

    def key_info(offset, length):
        key_pos = offset + jnp.arange(length, dtype=jnp.int32)
        inside = (key_pos >= 0) & (key_pos < total_rows)
        key_doc = lax.dynamic_slice_in_dim(all_docs, offset, length, 0)
        key_doc = jnp.where(inside, key_doc, -1)
        return (key_pos, key_doc)

    init_fwd = (
        jnp.full((head_count, shard_rows), very_low, jnp.float32),
        jnp.zeros((head_count, shard_rows), jnp.float32),
        jnp.zeros((head_count, shard_rows, HD), jnp.float32),
    )
    reach = min(4, seq_count - 1)
    near_keys = []
    near_keys.append((0, key_rows, value_rows))
    for distance in range(1, reach + 1):
        key_in, value_in = shifted((key_rows, value_rows), "seq", distance)
        near_keys.append((distance, key_in, value_in))
    running = init_fwd
    for distance, key_part, value_part in near_keys:
        forward_key_pos, forward_key_doc = key_info(
            first_row - distance * shard_rows, key_part.shape[0]
        )
        forward_run_max, forward_run_sum, forward_run_acc = running
        forward_scores, forward_allowed = pair_scores(
            query_rows, key_part, query_pos, forward_key_pos, doc_ids, forward_key_doc
        )
        forward_scores = jnp.where(forward_allowed, forward_scores, very_low)
        new_max = jnp.maximum(forward_run_max, jnp.max(forward_scores, axis=2))
        forward_attn_prob = jnp.where(
            forward_allowed, jnp.exp(forward_scores - new_max[:, :, None]), 0.0
        )
        factor = jnp.exp(forward_run_max - new_max)
        forward_run_sum = forward_run_sum * factor + jnp.sum(forward_attn_prob, axis=2)
        forward_run_acc = forward_run_acc * factor[:, :, None] + jnp.einsum(
            "hqk,khd->hqd",
            forward_attn_prob.astype(jnp.bfloat16),
            per_head(value_part),
            preferred_element_type=jnp.float32,
        )
        running = (new_max, forward_run_sum, forward_run_acc)
    run_max, run_sum, run_acc = running
    context = merged(run_acc / run_sum[:, :, None]).astype(jnp.bfloat16)
    log_total = run_max + jnp.log(run_sum)
    full_grad = lax.all_gather(grad_out, "heads", axis=1, tiled=True)
    grad_context = lax.dot_general(
        full_grad, out_weight, (((1,), (1,)), ((), ())), preferred_element_type=jnp.float32
    ).astype(jnp.bfloat16)
    weight_term = lax.dot_general(
        context, full_grad, (((0,), (0,)), ((), ())), preferred_element_type=jnp.float32
    )
    grad_weight = lax.psum_scatter(
        weight_term.astype(jnp.bfloat16), "seq", scatter_dimension=1, tiled=True
    ).astype(jnp.float32)
    row_delta = jnp.transpose(
        jnp.sum(
            per_head(grad_context).astype(jnp.float32) * per_head(context).astype(jnp.float32),
            axis=2,
        )
    )

    def owner_core(totals, query_part, grad_part, part_total, part_delta, offset):
        piece_rows = query_part.shape[0]
        piece_pos, piece_doc = key_info(offset, piece_rows)
        key_grad, value_grad = totals
        scores, allowed = pair_scores(
            query_part, key_rows, piece_pos, query_pos, piece_doc, doc_ids
        )
        attn_prob = jnp.where(allowed, jnp.exp(scores - part_total[:, :, None]), 0.0)
        grad_prob = jnp.einsum(
            "qhd,khd->hqk",
            per_head(grad_part),
            per_head(value_rows),
            preferred_element_type=jnp.float32,
        )
        grad_score = attn_prob * (grad_prob - part_delta[:, :, None])
        key_grad = key_grad + jnp.einsum(
            "hqk,qhd->hkd",
            grad_score.astype(jnp.bfloat16),
            per_head(query_part),
            preferred_element_type=jnp.float32,
        )
        value_grad = value_grad + jnp.einsum(
            "hqk,qhd->hkd",
            attn_prob.astype(jnp.bfloat16),
            per_head(grad_part),
            preferred_element_type=jnp.float32,
        )
        return (key_grad, value_grad)

    init_grad = jnp.zeros((head_count, shard_rows, HD), jnp.float32)
    query_acc = init_grad
    for distance, key_part, value_part in near_keys:
        query_key_pos, query_key_doc = key_info(
            first_row - distance * shard_rows, key_part.shape[0]
        )
        query_scores, query_allowed = pair_scores(
            query_rows, key_part, query_pos, query_key_pos, doc_ids, query_key_doc
        )
        query_attn_prob = jnp.where(
            query_allowed, jnp.exp(query_scores - log_total[:, :, None]), 0.0
        )
        query_grad_prob = jnp.einsum(
            "qhd,khd->hqk",
            per_head(grad_context),
            per_head(value_part),
            preferred_element_type=jnp.float32,
        )
        query_grad_score = query_attn_prob * (query_grad_prob - row_delta[:, :, None])
        query_acc = query_acc + jnp.einsum(
            "hqk,khd->hqd",
            query_grad_score.astype(jnp.bfloat16),
            per_head(key_part),
            preferred_element_type=jnp.float32,
        )
    owner_totals = owner_core(
        (init_grad, init_grad), query_rows, grad_context, log_total, row_delta, first_row
    )
    for distance in range(1, reach + 1):
        query_in, grad_in = shifted((query_rows, grad_context), "seq", -distance)
        total_in, delta_in = shifted((log_total, row_delta), "seq", -distance)
        owner_totals = owner_core(
            owner_totals, query_in, grad_in, total_in, delta_in, first_row + distance * shard_rows
        )
    key_acc, value_acc = owner_totals
    grad_keys = (merged(key_acc) * score_scale).astype(jnp.bfloat16)
    grad_values = merged(value_acc).astype(jnp.bfloat16)
    grad_query = (merged(query_acc) * score_scale).astype(jnp.bfloat16)
    return (grad_query, grad_keys, grad_values, grad_weight)


def solution(mesh):
    def shards(query_rows, *others):
        heads_here = query_rows.shape[1] // HD
        if heads_here == mesh.shape["seq"] == 2 * mesh.shape["heads"] == 8 and query_rows.shape[0] % BLOCK == 0:
            return head_shards(query_rows, *others)
        return ring_shards(query_rows, *others)

    return jax.shard_map(
        shards,
        mesh=mesh,
        in_specs=(
            P("seq", "heads"),
            P("seq", "heads"),
            P("seq", "heads"),
            P("seq"),
            P("seq", "heads"),
            P("heads", None),
        ),
        out_specs=(P("seq", "heads"), P("seq", "heads"), P("seq", "heads"), P("heads", "seq")),
        check_vma=False,
    )
```

```python
import functools
import math

import jax
import jax.numpy as jnp
from jax import lax
from jax.experimental import pallas as pl
from jax.experimental.pallas import tpu as pltpu
from jax.sharding import PartitionSpec as P

HD = 64


score_scale = 0.125
very_low = -1e30


def shifted(value, axis, by):
    devices = lax.axis_size(axis)
    pairs = [(i, i + by) for i in range(devices) if 0 <= i + by < devices]
    return lax.ppermute(value, axis, pairs)


def per_head(matrix):
    return matrix.reshape(matrix.shape[0], matrix.shape[1] // HD, HD)


def merged(tensor):
    return jnp.transpose(tensor, (1, 0, 2)).reshape(
        tensor.shape[1], tensor.shape[0] * tensor.shape[2]
    )


def pair_scores(query_part, key_part, query_pos, key_pos, query_doc, key_doc):
    scores = (
        jnp.einsum(
            "qhd,khd->hqk",
            per_head(query_part),
            per_head(key_part),
            preferred_element_type=jnp.float32,
        )
        * score_scale
    )
    allowed = (key_pos[None, :] <= query_pos[:, None]) & (key_doc[None, :] == query_doc[:, None])
    return (scores, allowed[None])


BLOCK = 512
MAX_DOC = 2048
LOG2E = math.log2(math.e)
EXP2_SCALE = score_scale * LOG2E
MESH = pl.DeviceIdType.MESH
VMEM = pl.BlockSpec(memory_space=pltpu.VMEM)
SMEM = pl.BlockSpec(memory_space=pltpu.SMEM)
HBM = pl.BlockSpec(memory_space=pl.ANY)


def mod(a, b):
    return lax.rem(a, jnp.int32(b))


def div(a, b):
    return lax.div(a, jnp.int32(b))


def greet(count, heads):
    me = lax.axis_index("seq")
    mine = lax.axis_index("heads")
    barrier = pltpu.get_barrier_semaphore()
    for step in range(1, count):
        pl.semaphore_signal(
            barrier, inc=1, device_id={"seq": mod(me + step, count)}, device_id_type=MESH
        )
    for step in range(1, heads):
        pl.semaphore_signal(
            barrier, inc=1, device_id={"heads": mod(mine + step, heads)}, device_id_type=MESH
        )
    pl.semaphore_wait(barrier, count - 1 + heads - 1)


def remote(src, dst, send, recv, slot, axis, peer):
    return pltpu.make_async_remote_copy(
        src_ref=src,
        dst_ref=dst,
        send_sem=send.at[slot],
        recv_sem=recv.at[slot],
        device_id={axis: peer},
        device_id_type=MESH,
    )


def head_rows(owner):
    return pl.ds(pl.multiple_of(owner * HD, HD), HD)


def token_cols(owner, cols):
    return pl.ds(pl.multiple_of(owner * cols, cols), cols)


def gather_kernel(
    count, heads, x_ref, doc_ref, grad_ref, weight_ref,
    qkv_ref, all_doc_ref, dctx_ref, full_ref,
    grads, dctx, xsend, xrecv, dsend, drecv, gsend, grecv, csend, crecv, local,
):
    me = lax.axis_index("seq")
    mine = lax.axis_index("heads")
    cols = x_ref.shape[2]
    width = grad_ref.shape[1]
    greet(count, heads)
    here = token_cols(me, cols)
    own = [
        pltpu.make_async_copy(grad_ref, grads.at[mine], local.at[0]),
        pltpu.make_async_copy(doc_ref, all_doc_ref.at[me], local.at[1]),
        pltpu.make_async_copy(x_ref.at[:, head_rows(me), :], qkv_ref.at[:, :, here], local.at[2]),
    ]
    for copy in own:
        copy.start()
    sibling = mine + 1 - 2 * mod(mine, 2)
    far = mod(mine + 2, 4)
    far_sibling = mod(sibling + 2, 4)
    wide = [
        remote(grad_ref, grads.at[mine], gsend, grecv, 0, "heads", far),
        remote(grad_ref, grads.at[mine], gsend, grecv, 1, "heads", sibling),
    ]
    peers = [mod(me + step, count) for step in range(1, count)]
    rest = [
        remote(doc_ref, all_doc_ref.at[me], dsend, drecv, step, "seq", peer)
        for step, peer in enumerate(peers)
    ] + [
        remote(
            x_ref.at[:, head_rows(peer), :], qkv_ref.at[:, :, here], xsend, xrecv, step, "seq", peer
        )
        for step, peer in enumerate(peers)
    ]
    for copy in wide + rest:
        copy.start()
    def product(part):
        at = pl.ds(pl.multiple_of(part * width, width), width)
        return nt_dot(weight_ref[:, at], grads[part])

    own[0].wait()
    total = product(mine)
    wide[0].wait()
    onward = remote(grads.at[far], grads.at[far], gsend, grecv, 2, "heads", sibling)
    onward.start()
    wide[1].wait()
    total = total + product(sibling) + product(far)
    onward.wait()
    keep = pltpu.make_async_copy(grads, full_ref, local.at[0])
    keep.start()
    total = total + product(far_sibling)
    dctx[...] = total.astype(jnp.bfloat16)
    last = [
        remote(dctx.at[head_rows(peer), :], dctx_ref.at[0, :, here], csend, crecv, step, "seq", peer)
        for step, peer in enumerate(peers)
    ]
    for copy in last:
        copy.start()
    own_dctx = pltpu.make_async_copy(dctx.at[head_rows(me), :], dctx_ref.at[0, :, here], local.at[3])
    own_dctx.start()
    for copy in own[1:] + rest + last:
        copy.wait()
    own_dctx.wait()
    keep.wait()


def gather(x, docs, grad_out, weight, count, heads):
    kinds, rows, cols = x.shape
    docs = docs.reshape(-1, 128)
    dma = pltpu.SemaphoreType.DMA
    return pl.pallas_call(
        functools.partial(gather_kernel, count, heads),
        out_shape=[
            jax.ShapeDtypeStruct((kinds, rows // count, cols * count), x.dtype),
            jax.ShapeDtypeStruct((count,) + docs.shape, docs.dtype),
            jax.ShapeDtypeStruct((1, rows // count, cols * count), x.dtype),
            jax.ShapeDtypeStruct((heads,) + grad_out.shape, grad_out.dtype),
        ],
        in_specs=[HBM, HBM, HBM, VMEM],
        out_specs=[HBM] * 4,
        scratch_shapes=[
            pltpu.VMEM((heads,) + grad_out.shape, grad_out.dtype),
            pltpu.VMEM((rows, cols), x.dtype),
        ]
        + [dma((count,))] * 4
        + [dma((heads,))] * 2
        + [dma((count,))] * 2
        + [dma((4,))],
        compiler_params=pltpu.CompilerParams(
            collective_id=0, has_side_effects=True, vmem_limit_bytes=40 << 20
        ),
    )(x, docs, grad_out, weight)


def return_kernel(
    count, x_ref, full_ref, back_ref, out_ref,
    ctx, own_sum, xout, xin, pout, pin, cout, cin,
    ksend, krecv, gsend, grecv, xsend, xrecv, psend, precv, csend, crecv, local,
):
    me = lax.axis_index("seq")
    z, x = div(me, 2), mod(me, 2)
    depth = count // 2
    cols = x_ref.shape[2] // count
    half = own_sum.shape[2]
    greet(count, 1)
    here = head_rows(me)
    own_ctx = pltpu.make_async_copy(
        x_ref.at[3, :, token_cols(me, cols)], ctx.at[here, :], local.at[0]
    )
    own_back = pltpu.make_async_copy(
        x_ref.at[0:3, :, token_cols(me, cols)], back_ref.at[:, here, :], local.at[1]
    )
    peers = [mod(me + step, count) for step in range(1, count)]
    first = [
        remote(x_ref.at[3, :, token_cols(peer, cols)], ctx.at[here, :], ksend, krecv, step, "seq", peer)
        for step, peer in enumerate(peers)
    ]
    grads = [
        remote(
            x_ref.at[0:3, :, token_cols(peer, cols)], back_ref.at[:, here, :],
            gsend, grecv, step, "seq", peer,
        )
        for step, peer in enumerate(peers)
    ]
    own_ctx.start()
    for copy in first:
        copy.start()
    own_back.start()
    own_ctx.wait()
    for copy in first:
        copy.wait()

    def product(part, side):
        at = pl.ds(pl.multiple_of(side * half, half), half)
        return jnp.dot(ctx[...], full_ref[part, :, at], preferred_element_type=jnp.float32)

    pair = z + 1 - 2 * mod(z, 2)
    far = mod(z + 2, 4)
    order = (mod(pair + 2, 4), pair, far, z)
    across = []
    for slot, part in enumerate(order):
        xout[slot] = product(part, 1 - x).astype(jnp.bfloat16)
        copy = remote(xout.at[slot], xin.at[slot], xsend, xrecv, slot, "seq", z * 2 + 1 - x)
        copy.start()
        across.append(copy)
    for copy in grads:
        copy.start()
    for slot, part in enumerate(order):
        own_sum[slot] = product(part, x)
    near = []
    for slot in range(2):
        across[slot].wait()
        pout[slot] = (own_sum[slot] + xin[slot].astype(jnp.float32)).astype(jnp.bfloat16)
        copy = remote(pout.at[slot], pin.at[slot], psend, precv, slot, "seq", pair * 2 + x)
        copy.start()
        near.append(copy)
    across[2].wait()
    near[0].wait()
    cout[...] = (
        own_sum[2] + xin[2].astype(jnp.float32) + pin[0].astype(jnp.float32)
    ).astype(jnp.bfloat16)
    cross = remote(cout, cin, csend, crecv, 0, "seq", far * 2 + x)
    cross.start()
    across[3].wait()
    near[1].wait()
    own_sum[3] += xin[3].astype(jnp.float32) + pin[1].astype(jnp.float32)
    cross.wait()
    out_ref[...] = own_sum[3] + cin[...].astype(jnp.float32)
    own_back.wait()
    for copy in grads:
        copy.wait()


def give_back(x, full, count):
    kinds, rows, tokens = x.shape
    inner, cols = rows * count, tokens // count
    depth = count // 2
    half = full.shape[2] // 2
    dma = pltpu.SemaphoreType.DMA
    bf16 = jnp.bfloat16
    block = (inner, half)
    return pl.pallas_call(
        functools.partial(return_kernel, count),
        out_shape=[
            jax.ShapeDtypeStruct((kinds - 1, inner, cols), x.dtype),
            jax.ShapeDtypeStruct(block, jnp.float32),
        ],
        in_specs=[HBM, VMEM],
        out_specs=[HBM, VMEM],
        scratch_shapes=[
            pltpu.VMEM((inner, cols), bf16),
            pltpu.VMEM((depth,) + block, jnp.float32),
            pltpu.VMEM((depth,) + block, bf16),
            pltpu.VMEM((depth,) + block, bf16),
            pltpu.VMEM((2,) + block, bf16),
            pltpu.VMEM((2,) + block, bf16),
            pltpu.VMEM(block, bf16),
            pltpu.VMEM(block, bf16),
        ]
        + [dma((count,))] * 4
        + [dma((depth,))] * 2
        + [dma((2,))] * 2
        + [dma((1,))] * 2
        + [dma((2,))],
        compiler_params=pltpu.CompilerParams(
            collective_id=1, has_side_effects=True, vmem_limit_bytes=40 << 20
        ),
    )(x, full)


def nt_dot(a, b):
    return lax.dot_general(a, b, (((1,), (1,)), ((), ())), preferred_element_type=jnp.float32)


def block_at(index):
    return pl.ds(pl.multiple_of(index * BLOCK, BLOCK), BLOCK)


def rows_of(cols_ref, slot, rows_ref, blocks):
    def step(b, _):
        at = block_at(b)
        rows_ref[at, :] = cols_ref[slot, :, at].T
        return 0

    lax.fori_loop(0, blocks, step, 0)


def attention_kernel(
    low_ref, full_ref, start_ref, qkv_ref, dctx_ref, out_ref,
    key_rows, value_rows, key_acc, value_acc, held_scores, held_prob,
):
    blocks = qkv_ref.shape[2] // BLOCK
    rows_of(qkv_ref, 1, key_rows, blocks)
    rows_of(qkv_ref, 2, value_rows, blocks)

    def query_block(j, _):
        cols = block_at(j)
        query_cols = qkv_ref[0, :, cols]
        start = start_ref[:, cols]
        low, full = low_ref[j], full_ref[j]

        def over_blocks(step, state):
            state = step(j, True, state)
            state = lax.fori_loop(low, full, lambda i, state: step(i, True, state), state)
            return lax.fori_loop(full, j, lambda i, state: step(i, False, state), state)

        def scores_step(i, masked, run_max):
            scores = jnp.dot(
                key_rows[block_at(i), :], query_cols, preferred_element_type=jnp.float32
            )
            if masked:
                key_pos = i * BLOCK + lax.broadcasted_iota(jnp.int32, scores.shape, 0)
                query_pos = j * BLOCK + lax.broadcasted_iota(jnp.int32, (1, BLOCK), 1)
                allowed = (key_pos <= query_pos) & (key_pos >= start)
                scores = jnp.where(allowed, scores, very_low)
            held_scores[i - low] = scores
            return jnp.maximum(run_max, jnp.max(scores, axis=0, keepdims=True))

        row_max = over_blocks(scores_step, jnp.full((1, BLOCK), very_low, jnp.float32))
        shift = row_max * EXP2_SCALE

        def context_step(i, state):
            run_sum, acc = state
            prob = jnp.exp2(held_scores[i - low] * EXP2_SCALE - shift)
            run_sum = run_sum + jnp.sum(prob, axis=0, keepdims=True)
            prob = prob.astype(jnp.bfloat16)
            held_prob[i - low] = prob
            acc = acc + jnp.dot(
                qkv_ref[2, :, block_at(i)], prob, preferred_element_type=jnp.float32
            )
            return run_sum, acc

        run_sum, acc = lax.fori_loop(
            low,
            j + 1,
            context_step,
            (jnp.zeros((1, BLOCK), jnp.float32), jnp.zeros((HD, BLOCK), jnp.float32)),
        )
        inverse = 1.0 / run_sum
        context = (acc * inverse).astype(jnp.bfloat16)
        out_ref[3, :, cols] = context
        grad_cols = (dctx_ref[0, :, cols].astype(jnp.float32) * inverse).astype(jnp.bfloat16)
        delta = jnp.sum(
            grad_cols.astype(jnp.float32) * context.astype(jnp.float32), axis=0, keepdims=True
        )

        def grads_step(i, query_acc):
            keys = block_at(i)
            prob = held_prob[i - low]
            grad_prob = jnp.dot(
                value_rows[keys, :], grad_cols, preferred_element_type=jnp.float32
            )
            grad_score = (prob.astype(jnp.float32) * (grad_prob - delta)).astype(jnp.bfloat16)
            value_acc[:, keys] += nt_dot(grad_cols, prob)
            key_acc[:, keys] += nt_dot(query_cols, grad_score)
            return query_acc + jnp.dot(
                qkv_ref[1, :, keys], grad_score, preferred_element_type=jnp.float32
            )

        key_acc[:, cols] = jnp.zeros((HD, BLOCK), jnp.float32)
        value_acc[:, cols] = jnp.zeros((HD, BLOCK), jnp.float32)
        query_acc = lax.fori_loop(
            low,
            j + 1,
            grads_step,
            jnp.zeros((HD, BLOCK), jnp.float32),
        )
        out_ref[0, :, cols] = (query_acc * score_scale).astype(jnp.bfloat16)
        return 0

    lax.fori_loop(0, blocks, query_block, 0)

    def finish(b, _):
        at = block_at(b)
        out_ref[1, :, at] = (key_acc[:, at] * score_scale).astype(jnp.bfloat16)
        out_ref[2, :, at] = value_acc[:, at].astype(jnp.bfloat16)
        return 0

    lax.fori_loop(0, blocks, finish, 0)


def attention(low, full, start, qkv, dctx):
    tokens = qkv.shape[2]
    reach = min(MAX_DOC // BLOCK + 1, tokens // BLOCK)
    return pl.pallas_call(
        attention_kernel,
        out_shape=jax.ShapeDtypeStruct((4, HD, tokens), jnp.bfloat16),
        in_specs=[SMEM, SMEM, VMEM, VMEM, VMEM],
        out_specs=VMEM,
        scratch_shapes=[pltpu.VMEM((tokens, HD), jnp.bfloat16)] * 2
        + [pltpu.VMEM((HD, tokens), jnp.float32)] * 2
        + [
            pltpu.VMEM((reach, BLOCK, BLOCK), jnp.float32),
            pltpu.VMEM((reach, BLOCK, BLOCK), jnp.bfloat16),
        ],
        compiler_params=pltpu.CompilerParams(vmem_limit_bytes=40 << 20),
    )(low, full, start, qkv, dctx)


def doc_ranges(docs):
    tokens = docs.shape[0]
    ids = jnp.arange(8, dtype=jnp.int32)
    begins = jnp.sum((docs[None, :] < ids[:, None]).astype(jnp.int32), axis=1)
    start = jnp.sum(jnp.where(docs[None, :] == ids[:, None], begins[:, None], 0), axis=0)
    blocks = tokens // BLOCK
    grouped = start.reshape(blocks, BLOCK)
    low = grouped[:, 0] // BLOCK
    full = (grouped[:, BLOCK - 1] + BLOCK - 1) // BLOCK
    full = jnp.minimum(full, jnp.arange(blocks, dtype=jnp.int32))
    return low, full, start[None]


def head_shards(query_rows, key_rows, value_rows, doc_ids, grad_out, out_weight):
    count = lax.axis_size("seq")
    stacked = jnp.stack([query_rows.T, key_rows.T, value_rows.T])
    qkv, docs, dctx, full_grad = gather(
        stacked, doc_ids, grad_out, out_weight, count, lax.axis_size("heads")
    )
    low, full, start = doc_ranges(docs.reshape(-1))
    results = attention(low, full, start, qkv, dctx)
    back, grad_weight = give_back(results, full_grad, count)
    return (back[0].T, back[1].T, back[2].T, grad_weight)


def ring_shards(query_rows, key_rows, value_rows, doc_ids, grad_out, out_weight):
    shard_rows = query_rows.shape[0]
    inner_cols = query_rows.shape[1]
    head_count = inner_cols // HD
    seq_count = lax.axis_size("seq")
    total_rows = shard_rows * seq_count
    first_row = lax.axis_index("seq") * shard_rows
    query_pos = first_row + jnp.arange(shard_rows, dtype=jnp.int32)
    all_docs = lax.all_gather(doc_ids, "seq", axis=0, tiled=True)

    def key_info(offset, length):
        key_pos = offset + jnp.arange(length, dtype=jnp.int32)
        inside = (key_pos >= 0) & (key_pos < total_rows)
        key_doc = lax.dynamic_slice_in_dim(all_docs, offset, length, 0)
        key_doc = jnp.where(inside, key_doc, -1)
        return (key_pos, key_doc)

    init_fwd = (
        jnp.full((head_count, shard_rows), very_low, jnp.float32),
        jnp.zeros((head_count, shard_rows), jnp.float32),
        jnp.zeros((head_count, shard_rows, HD), jnp.float32),
    )
    reach = min(4, seq_count - 1)
    near_keys = []
    near_keys.append((0, key_rows, value_rows))
    for distance in range(1, reach + 1):
        key_in, value_in = shifted((key_rows, value_rows), "seq", distance)
        near_keys.append((distance, key_in, value_in))
    running = init_fwd
    for distance, key_part, value_part in near_keys:
        forward_key_pos, forward_key_doc = key_info(
            first_row - distance * shard_rows, key_part.shape[0]
        )
        forward_run_max, forward_run_sum, forward_run_acc = running
        forward_scores, forward_allowed = pair_scores(
            query_rows, key_part, query_pos, forward_key_pos, doc_ids, forward_key_doc
        )
        forward_scores = jnp.where(forward_allowed, forward_scores, very_low)
        new_max = jnp.maximum(forward_run_max, jnp.max(forward_scores, axis=2))
        forward_attn_prob = jnp.where(
            forward_allowed, jnp.exp(forward_scores - new_max[:, :, None]), 0.0
        )
        factor = jnp.exp(forward_run_max - new_max)
        forward_run_sum = forward_run_sum * factor + jnp.sum(forward_attn_prob, axis=2)
        forward_run_acc = forward_run_acc * factor[:, :, None] + jnp.einsum(
            "hqk,khd->hqd",
            forward_attn_prob.astype(jnp.bfloat16),
            per_head(value_part),
            preferred_element_type=jnp.float32,
        )
        running = (new_max, forward_run_sum, forward_run_acc)
    run_max, run_sum, run_acc = running
    context = merged(run_acc / run_sum[:, :, None]).astype(jnp.bfloat16)
    log_total = run_max + jnp.log(run_sum)
    full_grad = lax.all_gather(grad_out, "heads", axis=1, tiled=True)
    grad_context = lax.dot_general(
        full_grad, out_weight, (((1,), (1,)), ((), ())), preferred_element_type=jnp.float32
    ).astype(jnp.bfloat16)
    weight_term = lax.dot_general(
        context, full_grad, (((0,), (0,)), ((), ())), preferred_element_type=jnp.float32
    )
    grad_weight = lax.psum_scatter(
        weight_term.astype(jnp.bfloat16), "seq", scatter_dimension=1, tiled=True
    ).astype(jnp.float32)
    row_delta = jnp.transpose(
        jnp.sum(
            per_head(grad_context).astype(jnp.float32) * per_head(context).astype(jnp.float32),
            axis=2,
        )
    )

    def owner_core(totals, query_part, grad_part, part_total, part_delta, offset):
        piece_rows = query_part.shape[0]
        piece_pos, piece_doc = key_info(offset, piece_rows)
        key_grad, value_grad = totals
        scores, allowed = pair_scores(
            query_part, key_rows, piece_pos, query_pos, piece_doc, doc_ids
        )
        attn_prob = jnp.where(allowed, jnp.exp(scores - part_total[:, :, None]), 0.0)
        grad_prob = jnp.einsum(
            "qhd,khd->hqk",
            per_head(grad_part),
            per_head(value_rows),
            preferred_element_type=jnp.float32,
        )
        grad_score = attn_prob * (grad_prob - part_delta[:, :, None])
        key_grad = key_grad + jnp.einsum(
            "hqk,qhd->hkd",
            grad_score.astype(jnp.bfloat16),
            per_head(query_part),
            preferred_element_type=jnp.float32,
        )
        value_grad = value_grad + jnp.einsum(
            "hqk,qhd->hkd",
            attn_prob.astype(jnp.bfloat16),
            per_head(grad_part),
            preferred_element_type=jnp.float32,
        )
        return (key_grad, value_grad)

    init_grad = jnp.zeros((head_count, shard_rows, HD), jnp.float32)
    query_acc = init_grad
    for distance, key_part, value_part in near_keys:
        query_key_pos, query_key_doc = key_info(
            first_row - distance * shard_rows, key_part.shape[0]
        )
        query_scores, query_allowed = pair_scores(
            query_rows, key_part, query_pos, query_key_pos, doc_ids, query_key_doc
        )
        query_attn_prob = jnp.where(
            query_allowed, jnp.exp(query_scores - log_total[:, :, None]), 0.0
        )
        query_grad_prob = jnp.einsum(
            "qhd,khd->hqk",
            per_head(grad_context),
            per_head(value_part),
            preferred_element_type=jnp.float32,
        )
        query_grad_score = query_attn_prob * (query_grad_prob - row_delta[:, :, None])
        query_acc = query_acc + jnp.einsum(
            "hqk,khd->hqd",
            query_grad_score.astype(jnp.bfloat16),
            per_head(key_part),
            preferred_element_type=jnp.float32,
        )
    owner_totals = owner_core(
        (init_grad, init_grad), query_rows, grad_context, log_total, row_delta, first_row
    )
    for distance in range(1, reach + 1):
        query_in, grad_in = shifted((query_rows, grad_context), "seq", -distance)
        total_in, delta_in = shifted((log_total, row_delta), "seq", -distance)
        owner_totals = owner_core(
            owner_totals, query_in, grad_in, total_in, delta_in, first_row + distance * shard_rows
        )
    key_acc, value_acc = owner_totals
    grad_keys = (merged(key_acc) * score_scale).astype(jnp.bfloat16)
    grad_values = merged(value_acc).astype(jnp.bfloat16)
    grad_query = (merged(query_acc) * score_scale).astype(jnp.bfloat16)
    return (grad_query, grad_keys, grad_values, grad_weight)


def solution(mesh):
    def shards(query_rows, *others):
        heads_here = query_rows.shape[1] // HD
        if heads_here == mesh.shape["seq"] == 2 * mesh.shape["heads"] == 8 and query_rows.shape[0] % BLOCK == 0:
            return head_shards(query_rows, *others)
        return ring_shards(query_rows, *others)

    return jax.shard_map(
        shards,
        mesh=mesh,
        in_specs=(
            P("seq", "heads"),
            P("seq", "heads"),
            P("seq", "heads"),
            P("seq"),
            P("seq", "heads"),
            P("heads", None),
        ),
        out_specs=(P("seq", "heads"), P("seq", "heads"), P("seq", "heads"), P("heads", "seq")),
        check_vma=False,
    )
```

```python
import functools
import math

import jax
import jax.numpy as jnp
from jax import lax
from jax.experimental import pallas as pl
from jax.experimental.pallas import tpu as pltpu
from jax.sharding import PartitionSpec as P

HD = 64


score_scale = 0.125
very_low = -1e30


def shifted(value, axis, by):
    devices = lax.axis_size(axis)
    pairs = [(i, i + by) for i in range(devices) if 0 <= i + by < devices]
    return lax.ppermute(value, axis, pairs)


def per_head(matrix):
    return matrix.reshape(matrix.shape[0], matrix.shape[1] // HD, HD)


def merged(tensor):
    return jnp.transpose(tensor, (1, 0, 2)).reshape(
        tensor.shape[1], tensor.shape[0] * tensor.shape[2]
    )


def pair_scores(query_part, key_part, query_pos, key_pos, query_doc, key_doc):
    scores = (
        jnp.einsum(
            "qhd,khd->hqk",
            per_head(query_part),
            per_head(key_part),
            preferred_element_type=jnp.float32,
        )
        * score_scale
    )
    allowed = (key_pos[None, :] <= query_pos[:, None]) & (key_doc[None, :] == query_doc[:, None])
    return (scores, allowed[None])


BLOCK = 512
MAX_DOC = 2048
LOG2E = math.log2(math.e)
EXP2_SCALE = score_scale * LOG2E
MESH = pl.DeviceIdType.MESH
VMEM = pl.BlockSpec(memory_space=pltpu.VMEM)
SMEM = pl.BlockSpec(memory_space=pltpu.SMEM)
HBM = pl.BlockSpec(memory_space=pl.ANY)


def mod(a, b):
    return lax.rem(a, jnp.int32(b))


def div(a, b):
    return lax.div(a, jnp.int32(b))


def greet(count, heads):
    me = lax.axis_index("seq")
    mine = lax.axis_index("heads")
    barrier = pltpu.get_barrier_semaphore()
    for step in range(1, count):
        pl.semaphore_signal(
            barrier, inc=1, device_id={"seq": mod(me + step, count)}, device_id_type=MESH
        )
    for step in range(1, heads):
        pl.semaphore_signal(
            barrier, inc=1, device_id={"heads": mod(mine + step, heads)}, device_id_type=MESH
        )
    pl.semaphore_wait(barrier, count - 1 + heads - 1)


def remote(src, dst, send, recv, slot, axis, peer):
    return pltpu.make_async_remote_copy(
        src_ref=src,
        dst_ref=dst,
        send_sem=send.at[slot],
        recv_sem=recv.at[slot],
        device_id={axis: peer},
        device_id_type=MESH,
    )


def head_rows(owner):
    return pl.ds(pl.multiple_of(owner * HD, HD), HD)


def token_cols(owner, cols):
    return pl.ds(pl.multiple_of(owner * cols, cols), cols)


def gather_kernel(
    count, heads, x_ref, doc_ref, grad_ref, weight_ref,
    qkv_ref, all_doc_ref, dctx_ref, full_ref,
    grads, dctx, xsend, xrecv, dsend, drecv, gsend, grecv, csend, crecv, local,
):
    me = lax.axis_index("seq")
    mine = lax.axis_index("heads")
    cols = x_ref.shape[2]
    width = grad_ref.shape[1]
    greet(count, heads)
    here = token_cols(me, cols)
    own = [
        pltpu.make_async_copy(grad_ref, grads.at[mine], local.at[0]),
        pltpu.make_async_copy(doc_ref, all_doc_ref.at[me], local.at[1]),
        pltpu.make_async_copy(x_ref.at[:, head_rows(me), :], qkv_ref.at[:, :, here], local.at[2]),
    ]
    for copy in own:
        copy.start()
    sibling = mine + 1 - 2 * mod(mine, 2)
    far = mod(mine + 2, 4)
    far_sibling = mod(sibling + 2, 4)
    wide = [
        remote(grad_ref, grads.at[mine], gsend, grecv, 0, "heads", far),
        remote(grad_ref, grads.at[mine], gsend, grecv, 1, "heads", sibling),
    ]
    steps = sorted(range(1, count), key=lambda step: abs(step - count // 2))
    peers = [mod(me + step, count) for step in steps]
    rest = [
        remote(doc_ref, all_doc_ref.at[me], dsend, drecv, step, "seq", peer)
        for step, peer in enumerate(peers)
    ] + [
        remote(
            x_ref.at[:, head_rows(peer), :], qkv_ref.at[:, :, here], xsend, xrecv, step, "seq", peer
        )
        for step, peer in enumerate(peers)
    ]
    for copy in wide + rest:
        copy.start()
    def product(part):
        at = pl.ds(pl.multiple_of(part * width, width), width)
        return nt_dot(weight_ref[:, at], grads[part])

    own[0].wait()
    total = product(mine)
    wide[0].wait()
    onward = remote(grads.at[far], grads.at[far], gsend, grecv, 2, "heads", sibling)
    onward.start()
    wide[1].wait()
    total = total + product(sibling) + product(far)
    onward.wait()
    keep = pltpu.make_async_copy(grads, full_ref, local.at[0])
    keep.start()
    total = total + product(far_sibling)
    dctx[...] = total.astype(jnp.bfloat16)
    last = [
        remote(dctx.at[head_rows(peer), :], dctx_ref.at[0, :, here], csend, crecv, step, "seq", peer)
        for step, peer in enumerate(peers)
    ]
    for copy in last:
        copy.start()
    own_dctx = pltpu.make_async_copy(dctx.at[head_rows(me), :], dctx_ref.at[0, :, here], local.at[3])
    own_dctx.start()
    for copy in own[1:] + rest + last:
        copy.wait()
    own_dctx.wait()
    keep.wait()


def gather(x, docs, grad_out, weight, count, heads):
    kinds, rows, cols = x.shape
    docs = docs.reshape(-1, 128)
    dma = pltpu.SemaphoreType.DMA
    return pl.pallas_call(
        functools.partial(gather_kernel, count, heads),
        out_shape=[
            jax.ShapeDtypeStruct((kinds, rows // count, cols * count), x.dtype),
            jax.ShapeDtypeStruct((count,) + docs.shape, docs.dtype),
            jax.ShapeDtypeStruct((1, rows // count, cols * count), x.dtype),
            jax.ShapeDtypeStruct((heads,) + grad_out.shape, grad_out.dtype),
        ],
        in_specs=[HBM, HBM, HBM, VMEM],
        out_specs=[HBM] * 4,
        scratch_shapes=[
            pltpu.VMEM((heads,) + grad_out.shape, grad_out.dtype),
            pltpu.VMEM((rows, cols), x.dtype),
        ]
        + [dma((count,))] * 4
        + [dma((heads,))] * 2
        + [dma((count,))] * 2
        + [dma((4,))],
        compiler_params=pltpu.CompilerParams(
            collective_id=0, has_side_effects=True, vmem_limit_bytes=40 << 20
        ),
    )(x, docs, grad_out, weight)


def return_kernel(
    count, x_ref, full_ref, back_ref, out_ref,
    ctx, own_sum, xout, xin, pout, pin, cout, cin,
    ksend, krecv, gsend, grecv, xsend, xrecv, psend, precv, csend, crecv, local,
):
    me = lax.axis_index("seq")
    z, x = div(me, 2), mod(me, 2)
    depth = count // 2
    cols = x_ref.shape[2] // count
    half = own_sum.shape[2]
    greet(count, 1)
    here = head_rows(me)
    own_ctx = pltpu.make_async_copy(
        x_ref.at[3, :, token_cols(me, cols)], ctx.at[here, :], local.at[0]
    )
    own_back = pltpu.make_async_copy(
        x_ref.at[0:3, :, token_cols(me, cols)], back_ref.at[:, here, :], local.at[1]
    )
    steps = sorted(range(1, count), key=lambda step: abs(step - count // 2))
    peers = [mod(me + step, count) for step in steps]
    first = [
        remote(x_ref.at[3, :, token_cols(peer, cols)], ctx.at[here, :], ksend, krecv, step, "seq", peer)
        for step, peer in enumerate(peers)
    ]
    grads = [
        remote(
            x_ref.at[0:3, :, token_cols(peer, cols)], back_ref.at[:, here, :],
            gsend, grecv, step, "seq", peer,
        )
        for step, peer in enumerate(peers)
    ]
    own_ctx.start()
    for copy in first:
        copy.start()
    own_back.start()
    own_ctx.wait()
    for copy in first:
        copy.wait()

    def product(part, side):
        at = pl.ds(pl.multiple_of(side * half, half), half)
        return jnp.dot(ctx[...], full_ref[part, :, at], preferred_element_type=jnp.float32)

    pair = z + 1 - 2 * mod(z, 2)
    far = mod(z + 2, 4)
    order = (mod(pair + 2, 4), pair, far, z)
    across = []
    for slot, part in enumerate(order):
        xout[slot] = product(part, 1 - x).astype(jnp.bfloat16)
        copy = remote(xout.at[slot], xin.at[slot], xsend, xrecv, slot, "seq", z * 2 + 1 - x)
        copy.start()
        across.append(copy)
    for copy in grads:
        copy.start()
    for slot, part in enumerate(order):
        own_sum[slot] = product(part, x)
    near = []
    for slot in range(2):
        across[slot].wait()
        pout[slot] = (own_sum[slot] + xin[slot].astype(jnp.float32)).astype(jnp.bfloat16)
        copy = remote(pout.at[slot], pin.at[slot], psend, precv, slot, "seq", pair * 2 + x)
        copy.start()
        near.append(copy)
    across[2].wait()
    near[0].wait()
    cout[...] = (
        own_sum[2] + xin[2].astype(jnp.float32) + pin[0].astype(jnp.float32)
    ).astype(jnp.bfloat16)
    cross = remote(cout, cin, csend, crecv, 0, "seq", far * 2 + x)
    cross.start()
    across[3].wait()
    near[1].wait()
    own_sum[3] += xin[3].astype(jnp.float32) + pin[1].astype(jnp.float32)
    cross.wait()
    out_ref[...] = own_sum[3] + cin[...].astype(jnp.float32)
    own_back.wait()
    for copy in grads:
        copy.wait()


def give_back(x, full, count):
    kinds, rows, tokens = x.shape
    inner, cols = rows * count, tokens // count
    depth = count // 2
    half = full.shape[2] // 2
    dma = pltpu.SemaphoreType.DMA
    bf16 = jnp.bfloat16
    block = (inner, half)
    return pl.pallas_call(
        functools.partial(return_kernel, count),
        out_shape=[
            jax.ShapeDtypeStruct((kinds - 1, inner, cols), x.dtype),
            jax.ShapeDtypeStruct(block, jnp.float32),
        ],
        in_specs=[HBM, VMEM],
        out_specs=[HBM, VMEM],
        scratch_shapes=[
            pltpu.VMEM((inner, cols), bf16),
            pltpu.VMEM((depth,) + block, jnp.float32),
            pltpu.VMEM((depth,) + block, bf16),
            pltpu.VMEM((depth,) + block, bf16),
            pltpu.VMEM((2,) + block, bf16),
            pltpu.VMEM((2,) + block, bf16),
            pltpu.VMEM(block, bf16),
            pltpu.VMEM(block, bf16),
        ]
        + [dma((count,))] * 4
        + [dma((depth,))] * 2
        + [dma((2,))] * 2
        + [dma((1,))] * 2
        + [dma((2,))],
        compiler_params=pltpu.CompilerParams(
            collective_id=1, has_side_effects=True, vmem_limit_bytes=40 << 20
        ),
    )(x, full)


def nt_dot(a, b):
    return lax.dot_general(a, b, (((1,), (1,)), ((), ())), preferred_element_type=jnp.float32)


def block_at(index):
    return pl.ds(pl.multiple_of(index * BLOCK, BLOCK), BLOCK)


def rows_of(cols_ref, slot, rows_ref, blocks):
    def step(b, _):
        at = block_at(b)
        rows_ref[at, :] = cols_ref[slot, :, at].T
        return 0

    lax.fori_loop(0, blocks, step, 0)


def in_pairs(low, high, step, state):
    pairs = lax.div(high - low, jnp.int32(2))
    middle = low + 2 * pairs

    def two(t, state):
        return step(low + 2 * t + 1, step(low + 2 * t, state))

    return lax.fori_loop(middle, high, step, lax.fori_loop(0, pairs, two, state))


def attention_kernel(
    low_ref, full_ref, start_ref, qkv_ref, dctx_ref, out_ref,
    key_rows, value_rows, key_acc, value_acc, held_scores, held_prob,
):
    blocks = qkv_ref.shape[2] // BLOCK
    rows_of(qkv_ref, 1, key_rows, blocks)
    rows_of(qkv_ref, 2, value_rows, blocks)

    def query_block(j, _):
        cols = block_at(j)
        query_cols = qkv_ref[0, :, cols]
        start = start_ref[:, cols]
        low, full = low_ref[j], full_ref[j]

        def over_blocks(step, state):
            state = step(j, True, state)
            state = lax.fori_loop(low, full, lambda i, state: step(i, True, state), state)
            return lax.fori_loop(full, j, lambda i, state: step(i, False, state), state)

        def scores_step(i, masked, run_max):
            scores = jnp.dot(
                key_rows[block_at(i), :], query_cols, preferred_element_type=jnp.float32
            )
            if masked:
                key_pos = i * BLOCK + lax.broadcasted_iota(jnp.int32, scores.shape, 0)
                query_pos = j * BLOCK + lax.broadcasted_iota(jnp.int32, (1, BLOCK), 1)
                allowed = (key_pos <= query_pos) & (key_pos >= start)
                scores = jnp.where(allowed, scores, very_low)
            held_scores[i - low] = scores
            return jnp.maximum(run_max, jnp.max(scores, axis=0, keepdims=True))

        row_max = over_blocks(scores_step, jnp.full((1, BLOCK), very_low, jnp.float32))
        shift = row_max * EXP2_SCALE

        def context_step(i, state):
            run_sum, acc = state
            prob = jnp.exp2(held_scores[i - low] * EXP2_SCALE - shift)
            run_sum = run_sum + jnp.sum(prob, axis=0, keepdims=True)
            prob = prob.astype(jnp.bfloat16)
            held_prob[i - low] = prob
            acc = acc + jnp.dot(
                qkv_ref[2, :, block_at(i)], prob, preferred_element_type=jnp.float32
            )
            return run_sum, acc

        run_sum, acc = in_pairs(
            low,
            j + 1,
            context_step,
            (jnp.zeros((1, BLOCK), jnp.float32), jnp.zeros((HD, BLOCK), jnp.float32)),
        )
        inverse = 1.0 / run_sum
        context = (acc * inverse).astype(jnp.bfloat16)
        out_ref[3, :, cols] = context
        grad_cols = (dctx_ref[0, :, cols].astype(jnp.float32) * inverse).astype(jnp.bfloat16)
        delta = jnp.sum(
            grad_cols.astype(jnp.float32) * context.astype(jnp.float32), axis=0, keepdims=True
        )

        def grads_step(i, query_acc):
            keys = block_at(i)
            prob = held_prob[i - low]
            grad_prob = jnp.dot(
                value_rows[keys, :], grad_cols, preferred_element_type=jnp.float32
            )
            grad_score = (prob.astype(jnp.float32) * (grad_prob - delta)).astype(jnp.bfloat16)
            value_acc[:, keys] += nt_dot(grad_cols, prob)
            key_acc[:, keys] += nt_dot(query_cols, grad_score)
            return query_acc + jnp.dot(
                qkv_ref[1, :, keys], grad_score, preferred_element_type=jnp.float32
            )

        key_acc[:, cols] = jnp.zeros((HD, BLOCK), jnp.float32)
        value_acc[:, cols] = jnp.zeros((HD, BLOCK), jnp.float32)
        query_acc = in_pairs(
            low,
            j + 1,
            grads_step,
            jnp.zeros((HD, BLOCK), jnp.float32),
        )
        out_ref[0, :, cols] = (query_acc * score_scale).astype(jnp.bfloat16)
        return 0

    lax.fori_loop(0, blocks, query_block, 0)

    def finish(b, _):
        at = block_at(b)
        out_ref[1, :, at] = (key_acc[:, at] * score_scale).astype(jnp.bfloat16)
        out_ref[2, :, at] = value_acc[:, at].astype(jnp.bfloat16)
        return 0

    lax.fori_loop(0, blocks, finish, 0)


def attention(low, full, start, qkv, dctx):
    tokens = qkv.shape[2]
    reach = min(MAX_DOC // BLOCK + 1, tokens // BLOCK)
    return pl.pallas_call(
        attention_kernel,
        out_shape=jax.ShapeDtypeStruct((4, HD, tokens), jnp.bfloat16),
        in_specs=[SMEM, SMEM, VMEM, VMEM, VMEM],
        out_specs=VMEM,
        scratch_shapes=[pltpu.VMEM((tokens, HD), jnp.bfloat16)] * 2
        + [pltpu.VMEM((HD, tokens), jnp.float32)] * 2
        + [
            pltpu.VMEM((reach, BLOCK, BLOCK), jnp.float32),
            pltpu.VMEM((reach, BLOCK, BLOCK), jnp.bfloat16),
        ],
        compiler_params=pltpu.CompilerParams(vmem_limit_bytes=40 << 20),
    )(low, full, start, qkv, dctx)


def doc_ranges(docs):
    tokens = docs.shape[0]
    ids = jnp.arange(8, dtype=jnp.int32)
    begins = jnp.sum((docs[None, :] < ids[:, None]).astype(jnp.int32), axis=1)
    start = jnp.sum(jnp.where(docs[None, :] == ids[:, None], begins[:, None], 0), axis=0)
    blocks = tokens // BLOCK
    grouped = start.reshape(blocks, BLOCK)
    low = grouped[:, 0] // BLOCK
    full = (grouped[:, BLOCK - 1] + BLOCK - 1) // BLOCK
    full = jnp.minimum(full, jnp.arange(blocks, dtype=jnp.int32))
    return low, full, start[None]


def head_shards(query_rows, key_rows, value_rows, doc_ids, grad_out, out_weight):
    count = lax.axis_size("seq")
    stacked = jnp.stack([query_rows.T, key_rows.T, value_rows.T])
    qkv, docs, dctx, full_grad = gather(
        stacked, doc_ids, grad_out, out_weight, count, lax.axis_size("heads")
    )
    low, full, start = doc_ranges(docs.reshape(-1))
    results = attention(low, full, start, qkv, dctx)
    back, grad_weight = give_back(results, full_grad, count)
    return (back[0].T, back[1].T, back[2].T, grad_weight)


def ring_shards(query_rows, key_rows, value_rows, doc_ids, grad_out, out_weight):
    shard_rows = query_rows.shape[0]
    inner_cols = query_rows.shape[1]
    head_count = inner_cols // HD
    seq_count = lax.axis_size("seq")
    total_rows = shard_rows * seq_count
    first_row = lax.axis_index("seq") * shard_rows
    query_pos = first_row + jnp.arange(shard_rows, dtype=jnp.int32)
    all_docs = lax.all_gather(doc_ids, "seq", axis=0, tiled=True)

    def key_info(offset, length):
        key_pos = offset + jnp.arange(length, dtype=jnp.int32)
        inside = (key_pos >= 0) & (key_pos < total_rows)
        key_doc = lax.dynamic_slice_in_dim(all_docs, offset, length, 0)
        key_doc = jnp.where(inside, key_doc, -1)
        return (key_pos, key_doc)

    init_fwd = (
        jnp.full((head_count, shard_rows), very_low, jnp.float32),
        jnp.zeros((head_count, shard_rows), jnp.float32),
        jnp.zeros((head_count, shard_rows, HD), jnp.float32),
    )
    reach = min(4, seq_count - 1)
    near_keys = []
    near_keys.append((0, key_rows, value_rows))
    for distance in range(1, reach + 1):
        key_in, value_in = shifted((key_rows, value_rows), "seq", distance)
        near_keys.append((distance, key_in, value_in))
    running = init_fwd
    for distance, key_part, value_part in near_keys:
        forward_key_pos, forward_key_doc = key_info(
            first_row - distance * shard_rows, key_part.shape[0]
        )
        forward_run_max, forward_run_sum, forward_run_acc = running
        forward_scores, forward_allowed = pair_scores(
            query_rows, key_part, query_pos, forward_key_pos, doc_ids, forward_key_doc
        )
        forward_scores = jnp.where(forward_allowed, forward_scores, very_low)
        new_max = jnp.maximum(forward_run_max, jnp.max(forward_scores, axis=2))
        forward_attn_prob = jnp.where(
            forward_allowed, jnp.exp(forward_scores - new_max[:, :, None]), 0.0
        )
        factor = jnp.exp(forward_run_max - new_max)
        forward_run_sum = forward_run_sum * factor + jnp.sum(forward_attn_prob, axis=2)
        forward_run_acc = forward_run_acc * factor[:, :, None] + jnp.einsum(
            "hqk,khd->hqd",
            forward_attn_prob.astype(jnp.bfloat16),
            per_head(value_part),
            preferred_element_type=jnp.float32,
        )
        running = (new_max, forward_run_sum, forward_run_acc)
    run_max, run_sum, run_acc = running
    context = merged(run_acc / run_sum[:, :, None]).astype(jnp.bfloat16)
    log_total = run_max + jnp.log(run_sum)
    full_grad = lax.all_gather(grad_out, "heads", axis=1, tiled=True)
    grad_context = lax.dot_general(
        full_grad, out_weight, (((1,), (1,)), ((), ())), preferred_element_type=jnp.float32
    ).astype(jnp.bfloat16)
    weight_term = lax.dot_general(
        context, full_grad, (((0,), (0,)), ((), ())), preferred_element_type=jnp.float32
    )
    grad_weight = lax.psum_scatter(
        weight_term.astype(jnp.bfloat16), "seq", scatter_dimension=1, tiled=True
    ).astype(jnp.float32)
    row_delta = jnp.transpose(
        jnp.sum(
            per_head(grad_context).astype(jnp.float32) * per_head(context).astype(jnp.float32),
            axis=2,
        )
    )

    def owner_core(totals, query_part, grad_part, part_total, part_delta, offset):
        piece_rows = query_part.shape[0]
        piece_pos, piece_doc = key_info(offset, piece_rows)
        key_grad, value_grad = totals
        scores, allowed = pair_scores(
            query_part, key_rows, piece_pos, query_pos, piece_doc, doc_ids
        )
        attn_prob = jnp.where(allowed, jnp.exp(scores - part_total[:, :, None]), 0.0)
        grad_prob = jnp.einsum(
            "qhd,khd->hqk",
            per_head(grad_part),
            per_head(value_rows),
            preferred_element_type=jnp.float32,
        )
        grad_score = attn_prob * (grad_prob - part_delta[:, :, None])
        key_grad = key_grad + jnp.einsum(
            "hqk,qhd->hkd",
            grad_score.astype(jnp.bfloat16),
            per_head(query_part),
            preferred_element_type=jnp.float32,
        )
        value_grad = value_grad + jnp.einsum(
            "hqk,qhd->hkd",
            attn_prob.astype(jnp.bfloat16),
            per_head(grad_part),
            preferred_element_type=jnp.float32,
        )
        return (key_grad, value_grad)

    init_grad = jnp.zeros((head_count, shard_rows, HD), jnp.float32)
    query_acc = init_grad
    for distance, key_part, value_part in near_keys:
        query_key_pos, query_key_doc = key_info(
            first_row - distance * shard_rows, key_part.shape[0]
        )
        query_scores, query_allowed = pair_scores(
            query_rows, key_part, query_pos, query_key_pos, doc_ids, query_key_doc
        )
        query_attn_prob = jnp.where(
            query_allowed, jnp.exp(query_scores - log_total[:, :, None]), 0.0
        )
        query_grad_prob = jnp.einsum(
            "qhd,khd->hqk",
            per_head(grad_context),
            per_head(value_part),
            preferred_element_type=jnp.float32,
        )
        query_grad_score = query_attn_prob * (query_grad_prob - row_delta[:, :, None])
        query_acc = query_acc + jnp.einsum(
            "hqk,khd->hqd",
            query_grad_score.astype(jnp.bfloat16),
            per_head(key_part),
            preferred_element_type=jnp.float32,
        )
    owner_totals = owner_core(
        (init_grad, init_grad), query_rows, grad_context, log_total, row_delta, first_row
    )
    for distance in range(1, reach + 1):
        query_in, grad_in = shifted((query_rows, grad_context), "seq", -distance)
        total_in, delta_in = shifted((log_total, row_delta), "seq", -distance)
        owner_totals = owner_core(
            owner_totals, query_in, grad_in, total_in, delta_in, first_row + distance * shard_rows
        )
    key_acc, value_acc = owner_totals
    grad_keys = (merged(key_acc) * score_scale).astype(jnp.bfloat16)
    grad_values = merged(value_acc).astype(jnp.bfloat16)
    grad_query = (merged(query_acc) * score_scale).astype(jnp.bfloat16)
    return (grad_query, grad_keys, grad_values, grad_weight)


def solution(mesh):
    def shards(query_rows, *others):
        heads_here = query_rows.shape[1] // HD
        if heads_here == mesh.shape["seq"] == 2 * mesh.shape["heads"] == 8 and query_rows.shape[0] % BLOCK == 0:
            return head_shards(query_rows, *others)
        return ring_shards(query_rows, *others)

    return jax.shard_map(
        shards,
        mesh=mesh,
        in_specs=(
            P("seq", "heads"),
            P("seq", "heads"),
            P("seq", "heads"),
            P("seq"),
            P("seq", "heads"),
            P("heads", None),
        ),
        out_specs=(P("seq", "heads"), P("seq", "heads"), P("seq", "heads"), P("heads", "seq")),
        check_vma=False,
    )
```
